128 devices in a mesh: grp: 2 (over y_lo), dom: 64 (over x, z, y_hi, core).
Axes of the slice: x: 4, y: 4 (y_hi: 2, y_lo: 2; y = y_hi * 2 + y_lo), z: 4, core: 2. Of those that a mesh axis runs over, the one named last changes fastest.
Arguments:
- atm_state: float32 [2, 16, 2048, 2048], P(None, None, ('grp', 'dom')), may hold values from -6 to 6
- ocean_state: float32 [2, 16, 512, 512], P(None, None, 'dom', 'grp'), may hold values from -6 to 6
- atm_levels: float32 [16, 16], replicated, may hold values from -1.5 to 1.5
- ocean_levels: float32 [16, 16], replicated, may hold values from -1.5 to 1.5
- tile_weight: bfloat16 [32768, 128, 128], P(('grp', 'dom')), may hold values from 0 to 0.049804688
- tile_owner: int32 [32768, 1], P(('grp', 'dom')), may hold values from 0 to 127; in each aligned block of 256 rows (0 to 255, 256 to 511, ...) at most 3 rows name the same one
- tile_block: int32 [32768], P(('grp', 'dom')), may hold values from 0 to 15
- tile_source: int32 [32768], P(('grp', 'dom')), may hold values from 0 to 255
- tile_count: int32 [128], P(('grp', 'dom')), may hold values from 128 to 256, as said below
Outputs:
- atm_final: float32 [2, 16, 2048, 2048], P(None, None, ('grp', 'dom'))
- ocean_final: float32 [2, 16, 512, 512], P(None, None, 'dom', 'grp')
The draws below stay inside these ranges and needn't reach their ends.
Inputs may be any that keep to these rules, and one draw needn't show every extreme that they name: `tile_owner`: among the 256 entries of one device's list, at most 3 name the same ocean device, live or not. `tile_count`: entries of a device's list at or past its count are padding and are ignored; some device's count is 256.
All inputs are finite; a program needn't handle non-finite values.
Results may differ from the reference program's by a relative error of at most 0.002.
Values may be sent and summed in bfloat16 or wider, within the bound.
No kernel may reach another device: no remote copies, remote signals or barrier semaphores. Data moves between devices by JAX's collectives and lax.ppermute only.
A program may use at most 128 MiB of HBM per device.

```python
import math
import jax
import jax.numpy as jnp
import numpy as np
from jax import lax

LEV = 16
NVAR = 2
STEPS = 4
YA = 2048
XO_DEV = 8
YO_DEV = 256
TPD = 256
CAP = 3
ABPD = 256
OBPD = 16
XA = 2048
XO = 512
YO = 512
N_GRP = 2
N_DOM = 64
DEVICES = 128


def draw_tile_count(key, part):
    key = jax.random.fold_in(key, 7)
    first, second = jax.random.split(key)
    counts = jax.random.randint(first, (DEVICES,), TPD // 2, TPD + 1)
    fullest = jax.random.randint(second, (), 0, DEVICES)
    return jnp.where(jnp.arange(DEVICES) == fullest, TPD, counts).astype(jnp.int32)


def plant(array, rng, smallest, top_value):
    dims = array.shape
    index_at = [jax.random.randint(jax.random.fold_in(rng, axis), (), 0, dims[axis]) for axis in range(len(dims))]
    array = array.at[tuple(index_at)].set(smallest)
    longest = dims.index(max(dims))
    index_at[longest] = (index_at[longest] + 1) % dims[longest]
    return array.at[tuple(index_at)].set(top_value)


def shard_levels(rng, dims, cuts, smallest, high):
    def one(dim, shards_of):
        draws = jax.random.uniform(jax.random.fold_in(jax.random.fold_in(rng, 6), dim), (shards_of,), jnp.float32, smallest / len(cuts), high / len(cuts))
        return jnp.repeat(jnp.exp(draws), dims[dim] // shards_of).reshape((-1,) + (1,) * (len(dims) - dim - 1))

    factor_of = one(*cuts[0])
    for cut in cuts[1:]:
        factor_of = factor_of * one(*cut)
    return factor_of


def deal_out(own_key, own, number, rows, number_of, top, most, slope):
    sequence = jax.random.permutation(own_key, number_of)
    packed, usual = load_shares(number_of, rows * top, most, slope, True), load_shares(number_of, rows * top, most, slope, False)
    places = jnp.arange(number_of)

    def named(sizes, offset_by):
        used = int((sizes > 0).sum())
        fixed = max(1, used // 4)
        moved = fixed + (places - fixed + offset_by * (used - fixed)) % max(1, number_of - fixed)
        return jnp.zeros((number_of,), jnp.int32).at[sequence[jnp.where(places < fixed, places, moved)]].set(jnp.asarray(sizes, jnp.int32))

    sizes = jnp.where(number % 4 == 0, named(packed, number // 4), named(usual, number - number // 4 - 1))
    mixed = jax.random.permutation(jax.random.fold_in(own, 3), number_of)
    source_of, sink = mixed[0:number_of // 2 * 2:2], mixed[1:number_of // 2 * 2:2]
    room = jnp.minimum(sizes[source_of] - 1, most - sizes[sink]) // 2
    room = jnp.where((source_of == sequence[0]) | (sink == sequence[0]) | (sizes[sink] == 0), 0, jnp.maximum(room, 0))
    moved = jax.random.randint(jax.random.fold_in(own, 4), (number_of // 2,), 0, 1 << 20) % (room + 1)
    sizes = sizes.at[source_of].add(-moved).at[sink].add(moved)
    items = jnp.searchsorted(jnp.cumsum(sizes), jnp.arange(rows * top), side="right").astype(jnp.int32)
    table = items.reshape(top, rows).T
    table = table[jax.random.permutation(jax.random.fold_in(own, 1), rows)]
    offset_by = jax.random.randint(jax.random.fold_in(own, 2), (rows, 1), 0, top)
    return jnp.take_along_axis(table, (jnp.arange(top)[None, :] + offset_by) % top, axis=1)


def load_shares(number_of, total, most, slope, full):
    portions = [(1 << 20) // math.isqrt(standing ** slope) + 1 for standing in range(1, number_of + 1)]
    largest = most if full else min(most, max(-(-total // number_of), total * portions[0] // sum(portions)))
    least = 1 if total - largest >= number_of - 1 else 0
    given, spare = [largest] + [least] * (number_of - 1), total - largest - least * (number_of - 1)
    while spare > 0:
        movable = [i for i in range(1, number_of) if given[i] < largest] or [i for i in range(1, number_of) if given[i] < most]
        pool, left = sum([portions[i] for i in movable]), spare
        for i in movable:
            addition = min(most - given[i], max(1, left * portions[i] // pool), spare)
            given[i] = given[i] + addition
            spare = spare - addition
    return np.array(given)


def scatter_about(rng, extent, width, reach, shards=(), held_as=jnp.bfloat16):
    drawn = jax.random.normal(rng, extent, jnp.float32) * width
    if len(shards) > 0:
        drawn = shard_levels(rng, extent, shards, -0.22, 0.18) * drawn
    return jnp.clip(drawn, min=-reach, max=reach).astype(held_as)


def setup_inputs(seed: int = 0) -> dict:
    key_of = jax.random.split(jax.random.key(seed), 10)
    atm_state = scatter_about(key_of[0], (NVAR, LEV, XA, YA), 1.0, 6.0, ((2, 128),), jnp.float32)
    ocean_state = scatter_about(key_of[1], (NVAR, LEV, XO, YO), 1.0, 6.0, ((2, 64), (3, 2)), jnp.float32)
    atm_levels = scatter_about(key_of[2], (LEV, LEV), LEV ** -0.5, 1.5, (), jnp.float32)
    ocean_levels = scatter_about(key_of[3], (LEV, LEV), LEV ** -0.5, 1.5, (), jnp.float32)
    tile_weight = jnp.clip(0.049804688 * jax.random.uniform(key_of[4], (DEVICES * TPD, 128, 128), jnp.float32) ** shard_levels(key_of[4], (DEVICES * TPD, 128, 128), ((0, 128),), -0.2, 0.2), 0.0, 0.049804688).astype(jnp.bfloat16)
    tile_owner_keys = jax.random.split(jax.random.fold_in(key_of[5], 1), (DEVICES * TPD) // TPD)
    tile_owner_turns = jax.random.permutation(jax.random.fold_in(key_of[5], 3), (DEVICES * TPD) // TPD)
    tile_owner = jax.vmap(lambda own, number: deal_out(jax.random.fold_in(key_of[5], 2), own, number, TPD, DEVICES, 1, CAP, 2))(tile_owner_keys, tile_owner_turns).reshape((DEVICES * TPD, 1))
    tile_block = plant(jax.random.randint(key_of[6], (DEVICES * TPD,), 0, OBPD), jax.random.fold_in(key_of[6], 1), 0, OBPD - 1).astype(jnp.int32)
    tile_source = plant(jax.random.randint(key_of[7], (DEVICES * TPD,), 0, ABPD), jax.random.fold_in(key_of[7], 1), 0, ABPD - 1).astype(jnp.int32)
    tile_count = draw_tile_count(jax.random.fold_in(key_of[9], 71), 0)
    return dict(atm_state=atm_state, ocean_state=ocean_state, atm_levels=atm_levels, ocean_levels=ocean_levels, tile_weight=tile_weight, tile_owner=tile_owner, tile_block=tile_block, tile_source=tile_source, tile_count=tile_count)


diffuse = 0.2
vertical = 0.25
couple = 0.5


def atmos_step(state, levels):
    along_x = jnp.roll(state, -1, axis=2) + jnp.roll(state, 1, axis=2)
    padded = jnp.pad(state, ((0, 0), (0, 0), (0, 0), (1, 1)))
    along_y = padded[..., 2:] + padded[..., :-2]
    mixing = jnp.einsum("lm,vmxy->vlxy", levels, state, precision=lax.Precision.HIGHEST)
    return state + diffuse * (along_x + along_y - 4.0 * state) + vertical * mixing


def ocean_step(state, levels):
    padded = jnp.pad(state, ((0, 0), (0, 0), (1, 1), (1, 1)))
    along_x = padded[:, :, 2:, 1:-1] + padded[:, :, :-2, 1:-1]
    along_y = padded[:, :, 1:-1, 2:] + padded[:, :, 1:-1, :-2]
    mixing = jnp.einsum("lm,vmxy->vlxy", levels, state, precision=lax.Precision.HIGHEST)
    return state + diffuse * (along_x + along_y - 4.0 * state) + vertical * mixing


def reference(atm_state, ocean_state, atm_levels, ocean_levels, tile_weight, tile_owner, tile_block, tile_source, tile_count):
    total = DEVICES * TPD
    surface = atm_state[:, 0].astype(jnp.bfloat16).reshape(NVAR, -1, 128).transpose(1, 0, 2)
    ocean_surface = ocean_state[:, 0].reshape(NVAR, N_DOM, XO_DEV, N_GRP, YO_DEV // 128, 128)
    ocean_blocks = ocean_surface.transpose(3, 1, 2, 4, 0, 5).reshape(DEVICES * OBPD, NVAR, 128)
    positions = jnp.arange(total, dtype=jnp.int32)
    alive = (positions % TPD) < jnp.repeat(tile_count, TPD)
    source = (positions // TPD) * ABPD + tile_source
    target = tile_owner[:, 0] * OBPD + tile_block
    weights = tile_weight.reshape(DEVICES, TPD, 128, 128)

    picked = surface[source].reshape(DEVICES, TPD, NVAR, 128)

    def forward(pair):
        return jnp.einsum("tfa,tao->tfo", pair[0].astype(jnp.float32), pair[1].astype(jnp.float32))

    forward_terms = lax.map(forward, (picked, weights)).reshape(total, NVAR, 128)
    forward_terms = jnp.where(alive[:, None, None], forward_terms, 0.0)
    received = jax.ops.segment_sum(forward_terms, target, num_segments=DEVICES * OBPD)
    flux = received - ocean_blocks
    flux_sent = flux.astype(jnp.bfloat16)

    flux_tiles = flux_sent[target].reshape(DEVICES, TPD, NVAR, 128)

    def backward(pair):
        return jnp.einsum("tfo,tao->tfa", pair[0].astype(jnp.float32), pair[1].astype(jnp.float32))

    back_terms = lax.map(backward, (flux_tiles, weights)).reshape(total, NVAR, 128)
    back_terms = jnp.where(alive[:, None, None], back_terms, 0.0)
    returned = jax.ops.segment_sum(back_terms, source, num_segments=DEVICES * ABPD)
    returned_field = returned.transpose(1, 0, 2).reshape(NVAR, XA, YA)

    flux_field = flux.reshape(N_GRP, N_DOM, XO_DEV, YO_DEV // 128, NVAR, 128)
    flux_field = flux_field.transpose(4, 1, 2, 0, 3, 5).reshape(NVAR, XO, YO)

    atmos = atm_state
    ocean = ocean_state
    for repeat in range(STEPS):
        atmos = atmos_step(atmos, atm_levels)
        ocean = ocean_step(ocean, ocean_levels)
    atm_final = atmos.at[:, 0].add(-couple * returned_field)
    ocean_final = ocean.at[:, 0].add(couple * flux_field)
    return atm_final, ocean_final
```

```python
import math

import jax
import jax.numpy as jnp
from jax import lax
from jax.experimental import pallas as pl
from jax.experimental.pallas import tpu as pltpu
from jax.sharding import PartitionSpec as P

STEPS = 4
HALO = STEPS
CAP = 3
ROWS = 8
LANES = 128
GROUP = 8
WIDE = 2048
RING = ("grp", "dom")
F32 = jnp.float32
BF16 = jnp.bfloat16

diffuse = 0.2
vertical = 0.25
couple = 0.5
MIB = 1 << 20


def params(mib, dims=1):
    return pltpu.CompilerParams(
        vmem_limit_bytes=mib * MIB, dimension_semantics=("arbitrary",) * dims
    )


def iota(shape, dim):
    return lax.broadcasted_iota(jnp.int32, shape, dim)


def onehot(mask):
    return jnp.where(mask, 1.0, 0.0).astype(BF16)


def split(value):
    high = value.astype(BF16)
    return high, (value - high.astype(F32)).astype(BF16)


def mxu(left, right, dims=((1,), (0,))):
    return lax.dot_general(left, right, (dims, ((), ())), preferred_element_type=F32)


def exact(left, right):
    return lax.dot_general(
        left, right, (((1,), (0,)), ((), ())), precision=lax.Precision.HIGHEST,
        preferred_element_type=F32,
    )


def column(row):
    n = row.shape[1]
    eye = iota((n, n), 0) == iota((n, n), 1)
    return jnp.sum(jnp.where(eye, jnp.broadcast_to(row, (n, n)), 0.0), axis=1, keepdims=True)


def pack_kernel(atm_ref, ocean_ref, next_ref, prev_ref):
    for ref, lanes in ((atm_ref, slice(0, WIDE)), (ocean_ref, slice(WIDE, None))):
        state = ref[0].astype(BF16)
        rows = state.shape[0]
        deep = rows // 16
        out = iota((16 * HALO, rows), 0)
        col = iota((16 * HALO, rows), 1)
        first = (out // HALO) * deep + out % HALO
        prev_ref[:, lanes] = mxu(onehot(col == first), state).astype(BF16)
        next_ref[:, lanes] = mxu(onehot(col == first + (deep - HALO)), state).astype(BF16)


def pack(atm, ocean):
    variables, rows, wide = atm.shape
    width = wide + ocean.shape[2]
    out = jax.ShapeDtypeStruct((variables * 16 * HALO, width), BF16)
    return pl.pallas_call(
        pack_kernel,
        grid=(variables,),
        in_specs=[
            pl.BlockSpec((1,) + atm.shape[1:], lambda v: (v, 0, 0)),
            pl.BlockSpec((1,) + ocean.shape[1:], lambda v: (v, 0, 0)),
        ],
        out_specs=[pl.BlockSpec((16 * HALO, width), lambda v: (v, 0))] * 2,
        out_shape=[out, out],
        compiler_params=params(24),
        name="pack_halo",
    )(atm, ocean)


def paths(order, distance):
    weights = [1]
    for _ in range(order):
        weights = [
            sum(weights[j] for j in (i - 2, i - 1, i) if 0 <= j < len(weights))
            for i in range(len(weights) + 2)
        ]
    total = 0.0
    for j in range(order + 1):
        total = jnp.where(distance == j, float(weights[order + j]), total)
    return total


def powers(levels):
    step = vertical * levels
    out = [None, step]
    for _ in range(STEPS - 1):
        out.append(exact(out[-1], step))
    return out


def operators(levels, own, image):
    rows, cols = 16 * own, 16 * own + 32 * HALO
    r, c = iota((rows, cols), 0), iota((rows, cols), 1)
    x = r % own
    inner = c < 16 * own
    past = c - 16 * own
    low = past < 16 * HALO
    m = jnp.where(inner, c // own, (past // HALO) % 16)
    xs = jnp.where(inner, c % own, jnp.where(low, past % HALO - HALO, own + past % HALO))
    same = r // own == m
    spread_r = jnp.where(iota((rows, LANES), 0) // own == iota((rows, LANES), 1), 1.0, 0.0)
    cc = iota((LANES, cols), 1)
    mm = jnp.where(cc < 16 * own, cc // own, ((cc - 16 * own) // HALO) % 16)
    spread_c = jnp.where(iota((LANES, cols), 0) == mm, 1.0, 0.0)
    mixed = [None if p is None else exact(exact(spread_r, p), spread_c) for p in powers(levels)]
    shifts = []
    for q in range(STEPS + 1):
        shift = paths(q, jnp.abs(xs - x))
        if image is not None:
            first, last = image
            mirror_low = jnp.where(first == 1, paths(q, jnp.abs(xs + x + 2)), 0.0)
            mirror_high = jnp.where(last == 1, paths(q, jnp.abs(2 * own - xs - x)), 0.0)
            shift = shift - mirror_low - mirror_high
            outside = ((first == 1) & (xs < 0)) | ((last == 1) & (xs >= own))
            shift = jnp.where(outside, 0.0, shift)
        shifts.append(shift)
    result = []
    for k in range(STEPS):
        total = 0.0
        for i in range(STEPS - k + 1):
            q = STEPS - k - i
            scale = math.comb(STEPS, k) * math.comb(STEPS - k, i) * diffuse ** (k + q)
            term = scale * shifts[q]
            total = total + (jnp.where(same, term, 0.0) if i == 0 else term * mixed[i])
        result.append(total)
    return result


def prepare_kernel(edge_ref, atm_levels_ref, ocean_levels_ref, atm_ref, ocean_ref):
    for k, matrix in enumerate(operators(atm_levels_ref[...], 16, None)):
        high, low = split(matrix)
        rows = pl.ds(k * 256, 256)
        atm_ref[rows, 0:256] = high[:, :256]
        atm_ref[rows, 256:512] = low[:, :256]
        atm_ref[rows, 512:768] = high[:, :256]
        atm_ref[rows, 768:896] = high[:, 256:]
        atm_ref[rows, 896:1024] = low[:, 256:]
    image = (edge_ref[1], edge_ref[2])
    for k, matrix in enumerate(operators(ocean_levels_ref[...], 8, image)):
        high, low = split(matrix)
        rows = pl.ds(k * 128, 128)
        ocean_ref[rows, 0:256] = high
        ocean_ref[rows, 256:512] = low
        ocean_ref[rows, 512:768] = high


def prepare(edge, atm_levels, ocean_levels):
    pad = ((0, LANES - 16), (0, LANES - 16))
    return pl.pallas_call(
        prepare_kernel,
        in_specs=[pl.BlockSpec(memory_space=pltpu.SMEM)]
        + [pl.BlockSpec(memory_space=pltpu.VMEM)] * 2,
        out_specs=[pl.BlockSpec(memory_space=pltpu.VMEM)] * 2,
        out_shape=[
            jax.ShapeDtypeStruct((1024, 1024), BF16),
            jax.ShapeDtypeStruct((512, 768), BF16),
        ],
        compiler_params=pltpu.CompilerParams(vmem_limit_bytes=24 * MIB),
        name="step_operators",
    )(edge, jnp.pad(atm_levels, pad), jnp.pad(ocean_levels, pad))


def neighbours_y(value):
    wide = value.shape[1]
    col = iota(value.shape, 1)
    before = jnp.where(col == 0, 0.0, pltpu.roll(value, 1, axis=1))
    after = jnp.where(col == wide - 1, 0.0, pltpu.roll(value, wide - 1, axis=1))
    return before + after


def atmos_kernel(x_ref, low_ref, high_ref, g_ref, *rest):
    out_ref, rhs, z = rest[-3:]
    state = x_ref[0]
    high, low = split(state)
    rhs[0:256] = high
    rhs[256:512] = high
    rhs[512:768] = low
    rhs[768:832] = low_ref[...]
    rhs[832:896] = high_ref[...]
    rhs[896:960] = low_ref[...]
    rhs[960:1024] = high_ref[...]
    for n in range(WIDE // 256):
        lanes = slice(n * 256, (n + 1) * 256)
        for k in range(STEPS):
            z[k, :, lanes] = mxu(g_ref[k * 256 : (k + 1) * 256], rhs[:, lanes])

    def sweep(tile, carry):
        rows = pl.ds(pl.multiple_of(tile * 8, 8), 8)
        total = x_ref[0, rows] * diffuse**STEPS
        for k in reversed(range(STEPS)):
            total = z[k, rows] + neighbours_y(total)
        out_ref[0, rows] = total
        return carry

    lax.fori_loop(0, 32, sweep, 0)


def atmos(v, atm, low, high, operator, earlier=None):
    specs = [
        pl.BlockSpec((1, 256, WIDE), lambda i: (v, 0, 0)),
        pl.BlockSpec((16 * HALO, WIDE), lambda i: (v, 0)),
        pl.BlockSpec((16 * HALO, WIDE), lambda i: (v, 0)),
        pl.BlockSpec((1024, 1024), lambda i: (0, 0)),
    ]
    operands = [atm, low, high, operator]
    if earlier is not None:
        specs.append(pl.BlockSpec(memory_space=pl.ANY))
        operands.append(earlier)
    return pl.pallas_call(
        atmos_kernel,
        grid=(1,),
        in_specs=specs,
        out_specs=pl.BlockSpec((1, 256, WIDE), lambda i: (v, 0, 0)),
        out_shape=jax.ShapeDtypeStruct(atm.shape, F32),
        scratch_shapes=[pltpu.VMEM((1024, WIDE), BF16), pltpu.VMEM((STEPS, 256, WIDE), F32)],
        input_output_aliases={} if earlier is None else {4: 0},
        compiler_params=params(40),
        cost_estimate=pl.CostEstimate(
            flops=2 * 1024 * 1024 * WIDE, bytes_accessed=7 * MIB, transcendentals=0
        ),
        name=f"atmosphere_{v}",
    )(*operands)


def edge_kernel(edge_ref, ocean_ref, low_ref, high_ref, out_ref):
    first = edge_ref[0] == 0
    for v in range(2):
        halo = slice(v * 16 * HALO, (v + 1) * 16 * HALO)
        own = ocean_ref[v].astype(BF16).astype(F32)
        parts = [own, low_ref[halo].astype(F32), high_ref[halo].astype(F32)]
        ext = jnp.concatenate(parts, axis=0)
        out_ref[v * 256 : (v + 1) * 256] = jnp.where(first, ext[:, 128:], ext[:, :128]).astype(BF16)


def edge_columns(edge, ocean, low, high):
    halo = pl.BlockSpec((32 * HALO, 256), lambda i: (0, WIDE // 256))
    return pl.pallas_call(
        edge_kernel,
        grid=(1,),
        in_specs=[
            pl.BlockSpec(memory_space=pltpu.SMEM),
            pl.BlockSpec(ocean.shape, lambda i: (0, 0, 0)),
            halo,
            halo,
        ],
        out_specs=pl.BlockSpec((512, 128), lambda i: (0, 0)),
        out_shape=jax.ShapeDtypeStruct((512, 128), BF16),
        compiler_params=params(16),
        name="ocean_edge",
    )(edge, ocean, low, high)


def ocean_kernel(edge_ref, ocean_ref, low_ref, high_ref, side_ref, g_ref, flux_ref, out_ref):
    first = edge_ref[0] == 0
    for v in range(2):
        halo = slice(v * 16 * HALO, (v + 1) * 16 * HALO)
        parts = [ocean_ref[v], low_ref[halo].astype(F32), high_ref[halo].astype(F32)]
        ext = jnp.concatenate(parts, axis=0)
        c0, c1 = ext[:, :128], ext[:, 128:]
        side = side_ref[v * 256 : (v + 1) * 256].astype(F32)
        wide = jnp.concatenate(
            [
                jnp.where(first, c0, side),
                jnp.where(first, c1, c0),
                jnp.where(first, side, c1),
            ],
            axis=1,
        )
        high, low = split(wide)
        z = mxu(g_ref[...], jnp.concatenate([high, high, low], axis=0))
        total = wide[:128] * diffuse**STEPS
        for k in reversed(range(STEPS)):
            total = z[k * 128 : (k + 1) * 128] + neighbours_y(total)
        left = jnp.where(first, total[:, :128], total[:, 128:256])
        right = jnp.where(first, total[:, 128:256], total[:, 256:])
        final = jnp.concatenate([left, right], axis=1)
        out_ref[v] = final
        out_ref[v, 0:8] = final[0:8] + couple * flux_ref[v]


def ocean_steps(edge, ocean, low, high, side, operator, flux):
    halo = pl.BlockSpec((32 * HALO, 256), lambda i: (0, WIDE // 256))
    return pl.pallas_call(
        ocean_kernel,
        grid=(1,),
        in_specs=[
            pl.BlockSpec(memory_space=pltpu.SMEM),
            pl.BlockSpec(ocean.shape, lambda i: (0, 0, 0)),
            halo,
            halo,
            pl.BlockSpec(side.shape, lambda i: (0, 0)),
            pl.BlockSpec(operator.shape, lambda i: (0, 0)),
            pl.BlockSpec(flux.shape, lambda i: (0, 0, 0)),
        ],
        out_specs=pl.BlockSpec(ocean.shape, lambda i: (0, 0, 0)),
        out_shape=jax.ShapeDtypeStruct(ocean.shape, F32),
        compiler_params=params(24),
        cost_estimate=pl.CostEstimate(
            flops=4 * 512 * 768 * 384, bytes_accessed=2 * MIB, transcendentals=0
        ),
        name="ocean",
    )(edge, ocean, low, high, side, operator, flux)


def masked(pair, i):
    return jnp.where(iota(pair.shape, 0) % GROUP == i, pair, 0.0)


def forward_kernel(
    count_ref, owner_ref, block_ref, source_ref, atm_ref, w_ref, out_ref, place_ref,
    picked, contrib,
):
    step, steps = pl.program_id(0), pl.num_programs(0)
    tiles = owner_ref.shape[1]
    per_row = WIDE // LANES

    @pl.when(step == 0)
    def _():
        source = source_ref[...]
        cell = (source % per_row) * 16 + source // per_row
        gather = onehot(iota((tiles, 256), 1).astype(F32) == column(cell.astype(F32)))
        for v in range(2):
            level = atm_ref[v].astype(BF16)
            blocks = [level[:, b * LANES : (b + 1) * LANES] for b in range(per_row)]
            picked[v] = mxu(gather, jnp.concatenate(blocks, axis=0))
        owner = owner_ref[...].astype(F32)
        earlier = (column(owner) == owner) & (
            iota((tiles, tiles), 0) < iota((tiles, tiles), 1)
        )
        rank = jnp.sum(jnp.where(earlier, 1.0, 0.0), axis=0, keepdims=True)
        live = iota((1, tiles), 1) < count_ref[0]
        place = owner_ref[...] * ROWS + rank.astype(jnp.int32)
        place_ref[0:1] = jnp.where(live, place, -64)
        place_ref[1:2] = jnp.where(live, owner_ref[...] * ROWS + 6, -64)
        place_ref[2:3] = jnp.where(live, cell, -64)
        block = block_ref[...]
        lane = rank * 16.0 + ((block % 2) * 8 + block // 2).astype(F32)
        place_ref[3:4] = lane.astype(jnp.int32)
        place_ref[4:8] = jnp.zeros((4, tiles), jnp.int32)

    held = w_ref.shape[0]
    for g in range(held // GROUP):
        rows = pl.ds(pl.multiple_of(step * held + g * GROUP, GROUP), GROUP)
        pair = jnp.concatenate([picked[0, rows], picked[1, rows]], axis=0)
        left = jnp.concatenate([masked(pair, i).astype(BF16) for i in range(GROUP)], axis=1)
        weights = w_ref[g * GROUP : (g + 1) * GROUP].reshape(GROUP * LANES, LANES)
        both = mxu(left, weights)
        contrib[0, rows] = both[:GROUP]
        contrib[1, rows] = both[GROUP:]

    @pl.when(step == steps - 1)
    def _():
        slots = out_ref.shape[0]
        row = iota((slots, tiles), 0)
        place = place_ref[0:1]
        left = jnp.concatenate(
            [onehot(row == place), onehot(row == place + CAP), onehot(row == place_ref[1:2])],
            axis=1,
        )
        lane = column(place_ref[3:4].astype(F32))
        names = onehot(iota((tiles, LANES), 1).astype(F32) == lane)
        first = jnp.concatenate(split(contrib[0]), axis=1)
        second = jnp.concatenate(split(contrib[1]), axis=1)
        third = jnp.concatenate([names, jnp.zeros_like(names)], axis=1)
        out = mxu(left, jnp.concatenate([first, second, third], axis=0))
        out_ref[...] = out[:, :LANES] + out[:, LANES:]


def forward(count, owner, block, source, atm, weights, devices, steps=4):
    tiles = weights.shape[0]
    row = pl.BlockSpec((1, tiles), lambda i: (0, 0))
    return pl.pallas_call(
        forward_kernel,
        grid=(steps,),
        in_specs=[
            pl.BlockSpec(memory_space=pltpu.SMEM),
            row,
            row,
            row,
            pl.BlockSpec((2, 16, WIDE), lambda i: (0, 0, 0)),
            pl.BlockSpec((tiles // steps, LANES, LANES), lambda i: (i, 0, 0)),
        ],
        out_specs=[
            pl.BlockSpec((devices * ROWS, LANES), lambda i: (0, 0)),
            pl.BlockSpec((8, tiles), lambda i: (0, 0)),
        ],
        out_shape=[
            jax.ShapeDtypeStruct((devices * ROWS, LANES), F32),
            jax.ShapeDtypeStruct((8, tiles), jnp.int32),
        ],
        scratch_shapes=[pltpu.VMEM((2, tiles, LANES), F32), pltpu.VMEM((2, tiles, LANES), F32)],
        compiler_params=params(32),
        cost_estimate=pl.CostEstimate(
            flops=32 * tiles * LANES * LANES, bytes_accessed=9 * MIB, transcendentals=0
        ),
        name="tiles_forward",
    )(count, owner, block, source, atm, weights)


def combine_kernel(inbox_ref, ocean_ref, out_ref, flux_ref):
    devices = inbox_ref.shape[0] // ROWS

    def plane(r):
        return pl.ds(r, devices, stride=ROWS)

    names = inbox_ref[plane(6), :]
    parts = []
    for r in range(2 * CAP):
        value = inbox_ref[plane(r), :]
        high, low = split(value)
        rest = (value - high.astype(F32) - low.astype(F32)).astype(BF16)
        parts += [high, low, rest]
    summed = mxu(names.T.astype(BF16), jnp.concatenate(parts, axis=1))
    fields = []
    for v in range(2):
        received = 0.0
        for k in range(CAP):
            rows = summed[k * 16 : (k + 1) * 16]
            for term in range(3):
                at = ((v * CAP + k) * 3 + term) * LANES
                received = received + rows[:, at : at + LANES]
        surface = ocean_ref[v]
        flux = received - jnp.concatenate([surface[:, :LANES], surface[:, LANES:]], axis=0)
        flux_ref[v] = jnp.concatenate([flux[:8], flux[8:]], axis=1)
        sent = flux.astype(BF16).astype(F32)
        empty = jnp.zeros_like(sent)
        for k in range(CAP):
            stack = [sent if j == k else empty for j in range(8)]
            fields.append(jnp.concatenate(stack, axis=0).astype(BF16))
    outgoing = mxu(names.astype(BF16), jnp.concatenate(fields, axis=1))
    for r in range(2 * CAP):
        out_ref[plane(r), :] = outgoing[:, r * LANES : (r + 1) * LANES]
    for r in range(2 * CAP, ROWS):
        out_ref[plane(r), :] = jnp.zeros((devices, LANES), F32)


def combine(inbox, ocean):
    return pl.pallas_call(
        combine_kernel,
        grid=(1,),
        in_specs=[
            pl.BlockSpec(inbox.shape, lambda i: (0, 0)),
            pl.BlockSpec((2, 8, 256), lambda i: (0, 0, 0)),
        ],
        out_specs=[
            pl.BlockSpec(inbox.shape, lambda i: (0, 0)),
            pl.BlockSpec((2, 8, 256), lambda i: (0, 0, 0)),
        ],
        out_shape=[
            jax.ShapeDtypeStruct(inbox.shape, F32),
            jax.ShapeDtypeStruct((2, 8, 256), F32),
        ],
        compiler_params=params(24),
        name="ocean_flux",
    )(inbox, ocean)


def backward_kernel(place_ref, inbox_ref, w_ref, atm_ref, out_ref, picked, terms):
    step, steps = pl.program_id(0), pl.num_programs(0)
    tiles = place_ref.shape[1]
    per_row = WIDE // LANES

    @pl.when(step == 0)
    def _():
        slots = inbox_ref.shape[0]
        place = column(place_ref[0:1].astype(F32)).astype(jnp.int32)
        inbox = inbox_ref[...].astype(BF16)
        slot = iota((tiles, slots), 1)
        for v in range(2):
            picked[v] = mxu(onehot(slot == place + v * CAP), inbox)

    held = w_ref.shape[0]
    for g in range(held // GROUP):
        rows = pl.ds(pl.multiple_of(step * held + g * GROUP, GROUP), GROUP)
        pair = jnp.concatenate([picked[0, rows], picked[1, rows]], axis=0)
        weights = w_ref[g * GROUP : (g + 1) * GROUP].reshape(GROUP * LANES, LANES)
        wide = mxu(pair.astype(BF16), weights, ((1,), (1,)))
        both = 0.0
        for i in range(GROUP):
            both = both + masked(wide[:, i * LANES : (i + 1) * LANES], i)
        terms[0, rows] = both[:GROUP]
        terms[1, rows] = both[GROUP:]

    @pl.when(step == steps - 1)
    def _():
        scatter = onehot(iota((256, tiles), 0) == place_ref[2:3])
        halves = [part for v in range(2) for part in split(terms[v])]
        summed = mxu(scatter, jnp.concatenate(halves, axis=1))
        for v in range(2):
            at = 2 * v * LANES
            returned = summed[:, at : at + LANES] + summed[:, at + LANES : at + 2 * LANES]
            for b in range(per_row):
                lanes = slice(b * LANES, (b + 1) * LANES)
                out_ref[v, :, lanes] = (
                    atm_ref[v, :, lanes] - couple * returned[b * 16 : (b + 1) * 16]
                )


def backward(place, inbox, weights, atm, steps=4):
    tiles = weights.shape[0]
    level = pl.BlockSpec((2, 16, WIDE), lambda i: (0, 0, 0))
    return pl.pallas_call(
        backward_kernel,
        grid=(steps,),
        in_specs=[
            pl.BlockSpec(place.shape, lambda i: (0, 0)),
            pl.BlockSpec(inbox.shape, lambda i: (0, 0)),
            pl.BlockSpec((tiles // steps, LANES, LANES), lambda i: (i, 0, 0)),
            level,
        ],
        out_specs=level,
        out_shape=jax.ShapeDtypeStruct(atm.shape, F32),
        scratch_shapes=[pltpu.VMEM((2, tiles, LANES), F32), pltpu.VMEM((2, tiles, LANES), F32)],
        input_output_aliases={3: 0},
        compiler_params=params(32),
        cost_estimate=pl.CostEstimate(
            flops=32 * tiles * LANES * LANES, bytes_accessed=9 * MIB, transcendentals=0
        ),
        name="tiles_backward",
    )(place, inbox, weights, atm)


def swap(rows):
    devices = lax.axis_size(RING)
    boxes = rows.reshape(devices, ROWS, LANES)
    return lax.all_to_all(boxes, RING, split_axis=0, concat_axis=0, tiled=True).reshape(rows.shape)


def per_device(
    atm_state,
    ocean_state,
    atm_levels,
    ocean_levels,
    tile_weight,
    tile_owner,
    tile_block,
    tile_source,
    tile_count,
):
    devices = lax.axis_size(RING)
    tiles = tile_weight.shape[0]
    atm = atm_state.reshape(2, 256, WIDE)
    ocean = ocean_state.reshape(2, 128, 256)
    grp, dom = lax.axis_index("grp"), lax.axis_index("dom")
    last = lax.axis_size("dom") - 1
    edge = jnp.stack([grp, (dom == 0).astype(jnp.int32), (dom == last).astype(jnp.int32)])

    to_next, to_prev = pack(atm, ocean)
    forth = [(i, (i + 1) % devices) for i in range(devices)]
    back = [(target, source) for source, target in forth]
    low = lax.ppermute(to_next, RING, forth)
    high = lax.ppermute(to_prev, RING, back)

    outbox, place = forward(
        tile_count, tile_owner.reshape(1, tiles), tile_block.reshape(1, tiles),
        tile_source.reshape(1, tiles), atm, tile_weight, devices,
    )
    inbox = swap(outbox)
    atm_operator, ocean_operator = prepare(edge, atm_levels, ocean_levels)
    half = atmos(0, atm, low, high, atm_operator)
    columns = edge_columns(edge, ocean, low, high)
    side = lax.ppermute(columns, "grp", [(0, 1), (1, 0)])
    outgoing, flux = combine(inbox, ocean)
    returned = swap(outgoing)
    whole = atmos(1, atm, low, high, atm_operator, half)
    ocean_final = ocean_steps(edge, ocean, low, high, side, ocean_operator, flux)
    atm_final = backward(place, returned, tile_weight, whole)
    return atm_final.reshape(atm_state.shape), ocean_final.reshape(ocean_state.shape)


def solution(mesh):
    in_specs = (
        P(None, None, RING, None),
        P(None, None, "dom", "grp"),
        P(),
        P(),
        P(RING, None, None),
        P(RING, None),
        P(RING),
        P(RING),
        P(RING),
    )
    out_specs = (P(None, None, RING, None), P(None, None, "dom", "grp"))
    return jax.shard_map(
        per_device, mesh=mesh, in_specs=in_specs, out_specs=out_specs, check_vma=False
    )
```

```python
import functools
import math

import jax
import jax.numpy as jnp
from jax import lax
from jax.experimental import pallas as pl
from jax.experimental.pallas import tpu as pltpu
from jax.sharding import PartitionSpec as P

STEPS = 4
HALO = STEPS
CAP = 3
ROWS = 8
LANES = 128
GROUP = 8
PAD = 8
WIDE = 2048
RING = ("grp", "dom")
F32 = jnp.float32
BF16 = jnp.bfloat16

diffuse = 0.2
vertical = 0.25
couple = 0.5
MIB = 1 << 20


VMEM = pl.BlockSpec(memory_space=pltpu.VMEM)
HBM = pl.BlockSpec(memory_space=pltpu.HBM)
SMEM = pl.BlockSpec(memory_space=pltpu.SMEM)


def params(mib):
    return pltpu.CompilerParams(vmem_limit_bytes=mib * MIB)


def cost(flops, mib):
    return pl.CostEstimate(flops=flops, bytes_accessed=mib * MIB, transcendentals=0)


def fetch(pairs, sems):
    copies = []
    for n, (source, target) in enumerate(pairs):
        copies.append(pltpu.make_async_copy(source, target, sems.at[n]))
        copies[-1].start()
    return copies


def iota(shape, dim):
    return lax.broadcasted_iota(jnp.int32, shape, dim)


def onehot(mask):
    return jnp.where(mask, 1.0, 0.0).astype(BF16)


def split(value):
    high = value.astype(BF16)
    return high, (value - high.astype(F32)).astype(BF16)


def mxu(left, right, dims=((1,), (0,))):
    return lax.dot_general(left, right, (dims, ((), ())), preferred_element_type=F32)


def exact(left, right):
    return lax.dot_general(
        left, right, (((1,), (0,)), ((), ())), precision=lax.Precision.HIGHEST,
        preferred_element_type=F32,
    )


def column(row):
    n = row.shape[1]
    eye = iota((n, n), 0) == iota((n, n), 1)
    return jnp.sum(jnp.where(eye, jnp.broadcast_to(row, (n, n)), 0.0), axis=1, keepdims=True)


def select_rows(state, offset):
    rows = state.shape[0]
    deep = rows // 16
    out, col = iota((16 * HALO, rows), 0), iota((16 * HALO, rows), 1)
    return mxu(onehot(col == (out >> 2) * deep + (out & 3) + offset % deep), state)


def coefficients():
    table = []
    for s in range(STEPS):
        by_level = []
        for i in range(STEPS - s + 1):
            by_distance = [0.0] * (STEPS + 1)
            for k in range(s, STEPS - i + 1, 2):
                q = STEPS - k - i
                trinomial = [1]
                for _ in range(q):
                    padded = [0, 0] + trinomial + [0, 0]
                    trinomial = [sum(padded[j : j + 3]) for j in range(len(trinomial) + 2)]
                scale = math.comb(k, (k - s) // 2) * math.comb(STEPS, k)
                scale *= math.comb(STEPS - k, i) * diffuse ** (k + q)
                for d in range(q + 1):
                    by_distance[d] += scale * trinomial[q + d]
            by_level.append(by_distance)
        table.append(by_level)
    return table


def lookup(weights, distance):
    total = 0.0
    for d, weight in enumerate(weights):
        if weight:
            total = jnp.where(distance == d, weight, total)
    return total


def stencils(own, image):
    table = coefficients()
    x = iota((16, LANES), 1) & (own - 1)
    r = iota((16, LANES), 0)
    sources = [(r & (own - 1), own), ((r & 3) - HALO, HALO), ((r & 3) + own, HALO)]
    result = [[[] for _ in by_level] for by_level in table]
    for xs, depth in sources:
        distance = jnp.abs(xs - x)
        if image is not None:
            first, last = image
            below = jnp.where(first == 1, jnp.abs(xs + x + 2), STEPS + 1)
            above = jnp.where(last == 1, jnp.abs(2 * own - xs - x), STEPS + 1)
            inside = ((first == 0) | (xs >= 0)) & ((last == 0) | (xs < own))
        for s, by_level in enumerate(table):
            for i, weights in enumerate(by_level):
                part = lookup(weights, distance)
                if image is not None:
                    part = part - lookup(weights, below) - lookup(weights, above)
                    part = jnp.where(inside, part, 0.0)
                result[s][i] += [part] * depth
    return [[jnp.concatenate(parts, axis=0) for parts in by_level] for by_level in result]


def small_product(left, right):
    total = 0.0
    for k in range(16):
        total = total + left[:, k : k + 1] * right[k : k + 1, :]
    return total


def operators(levels, own, image):
    rows, cols = 16 * own + 32 * HALO, 16 * own
    shift = own.bit_length() - 1
    one = vertical * levels.T[:16]
    two = small_product(one, one)
    stack = [half for p in (one, two, small_product(two, one), small_product(two, two))
             for half in split(p)]
    stack = jnp.concatenate([half.astype(F32) for half in stack], axis=0).astype(BF16)
    spread = onehot(iota((LANES, cols), 0) == (iota((LANES, cols), 1) >> shift))
    wide = mxu(stack, spread).astype(BF16)
    r, c = iota((rows, LANES), 0), iota((rows, LANES), 1)
    level = jnp.where(r < cols, r >> shift, (r >> 2) & 15)
    mixed = [mxu(onehot(((c & 15) == level) & ((c >> 5) == i)), wide) for i in range(STEPS)]
    r, c = iota((rows, cols), 0), iota((rows, cols), 1)
    same = jnp.where(r < cols, r >> shift, (r >> 2) & 15) == (c >> shift)
    result = []
    for by_level in stencils(own, image):
        total = 0.0
        for i, part in enumerate(by_level):
            part = jnp.concatenate([part] * (cols // LANES), axis=1)
            total = total + (jnp.where(same, part, 0.0) if i == 0 else part * mixed[i - 1])
        result.append(total)
    return result


def write_operators(edge_ref, levels, own_ref, halo_ref, ocean_ref):
    for s, part in enumerate(operators(levels[0], 16, None)):
        high, low = split(part[:256])
        lanes = slice((s & 1) * 256, (s & 1) * 256 + 256)
        if s < 2:
            own_ref[0:256, lanes] = low
            own_ref[256:512, lanes] = high
        else:
            own_ref[512:768, lanes] = high
        halo_ref[:, s * 256 : (s + 1) * 256] = part[256:].astype(BF16)
    image = (edge_ref[1], edge_ref[2])
    for s, part in enumerate(operators(levels[1], 8, image)):
        lanes = slice(s * LANES, (s + 1) * LANES)
        high, low = split(part[:128])
        ocean_ref[0:128, lanes] = low
        ocean_ref[128:256, lanes] = high
        ocean_ref[256:384, lanes] = part[128:].astype(BF16)


OWN, FAR, SEA = (768, 512), (128, 1024), (384, 512)


def mirror_low(rows):
    r = iota(rows.shape, 0)
    total = jnp.zeros_like(rows)
    for j in range(3):
        total = jnp.where(r == 6 - j, -rows[j : j + 1], total)
    return total


def mirror_high(rows):
    r = iota(rows.shape, 0)
    total = jnp.zeros_like(rows)
    for j in range(3):
        total = jnp.where(r == 1 + j, -rows[7 - j : 8 - j], total)
    return total


def halo_rows(halo, v):
    half = 16 * HALO
    empty = jnp.zeros((half, halo.shape[1]), halo.dtype)
    blocks = []
    for side in range(2):
        part = halo[side * half : (side + 1) * half]
        blocks += [part, empty] if v == 0 else [empty, part]
    return jnp.concatenate(blocks, axis=0)


def atmos_steps(v, arrivals, x_ref, low_ref, high_ref, own_ref, halo_ref, out_ref, surface_ref,
                left, main, minor, w, held, sems):
    chunks = len(arrivals)
    size = WIDE // chunks
    main[0:512] = own_ref[0:512]
    main[512:768] = own_ref[256:512]
    main[768:1024] = halo_rows(halo_ref[:, 0:512], v)
    minor[0:256] = own_ref[512:768]
    minor[256:512] = halo_rows(halo_ref[:, 512:1024], v)
    copies = []
    for n in range(chunks + 1):
        if n < chunks:
            arrivals[n].wait()
            start = n * size
            for c in range(size // LANES):
                rows = slice(c * LANES, (c + 1) * LANES)
                at = start + c * LANES
                for h in range(2):
                    state = x_ref[h * LANES : (h + 1) * LANES, at : at + LANES].T
                    high, low = split(state)
                    lanes = slice(h * LANES, (h + 1) * LANES)
                    w[STEPS, PAD + at : PAD + at + LANES, lanes] = state * diffuse**STEPS
                    left[rows, h * LANES : (h + 1) * LANES] = high
                    left[rows, 256 + h * LANES : 256 + (h + 1) * LANES] = low
                    left[rows, 512 + h * LANES : 512 + (h + 1) * LANES] = high
            left[:, 768:896] = low_ref[start : start + size]
            left[:, 896:1024] = high_ref[start : start + size]
            rows = slice(PAD + start, PAD + start + size)
            for s in range(2):
                lanes = slice(s * 256, (s + 1) * 256)
                w[s, rows] = mxu(left[...], main[:, lanes])
                w[2 + s, rows] = mxu(left[:, 512:1024], minor[:, lanes])
        if n == 0:
            for s in range(1, STEPS + 1):
                w[s, 0:PAD] = mirror_low(w[s, PAD : 2 * PAD])
        if n == chunks - 1:
            for s in range(1, STEPS + 1):
                w[s, WIDE + PAD : WIDE + 2 * PAD] = mirror_high(w[s, WIDE : WIDE + PAD])
        if n > 0:
            start = (n - 1) * size
            for c in range(size // LANES):
                at = PAD + start + c * LANES
                for h in range(2):
                    lanes = slice(h * LANES, (h + 1) * LANES)
                    total = w[0, at : at + LANES, lanes]
                    for s in range(1, STEPS + 1):
                        total += w[s, at - s : at - s + LANES, lanes]
                        total += w[s, at + s : at + s + LANES, lanes]
                    held[lanes, at - PAD : at - PAD + LANES] = total.T
            cells = pl.ds(start, size)
            surface_ref[:, start : start + size] = held[0:16, start : start + size]
            copy = pltpu.make_async_copy(
                held.at[:, cells], out_ref.at[v, :, cells], sems.at[n - 1]
            )
            copy.start()
            copies.append(copy)
    return copies


def atmos_scratch(chunks):
    size = WIDE // chunks
    return [
        pltpu.VMEM((256, WIDE), F32),
        pltpu.SemaphoreType.DMA((chunks,)),
        pltpu.VMEM((size, 1024), BF16),
        pltpu.VMEM((1024, 512), BF16),
        pltpu.VMEM((512, 512), BF16),
        pltpu.VMEM((STEPS + 1, WIDE + 2 * PAD, 256), F32),
        pltpu.VMEM((256, WIDE), F32),
        pltpu.SemaphoreType.DMA((chunks,)),
    ]


def fetch_atmos(v, atm_ref, x_ref, sems):
    size = WIDE // sems.shape[0]
    cells = [pl.ds(n * size, size) for n in range(sems.shape[0])]
    return fetch([(atm_ref.at[v, :, c], x_ref.at[:, c]) for c in cells], sems)


def edge_kernel(edge_ref, ocean_ref, low_ref, high_ref, out_ref):
    first = edge_ref[0] == 0
    for v in range(2):
        before, after = ocean_ref[v, :, 0:LANES].T[:PAD], ocean_ref[v, :, LANES:].T[LANES - PAD :]
        out_ref[v * PAD : (v + 1) * PAD] = jnp.where(first, after, before)
    for n, ref in enumerate((low_ref, high_ref)):
        before, after = ref[WIDE : WIDE + 16], ref[WIDE + 240 : WIDE + 256]
        edge = jnp.where(first, after.astype(F32)[16 - PAD :], before.astype(F32)[:PAD])
        out_ref[(2 + n) * PAD : (3 + n) * PAD] = edge


def edge_rows(edge, ocean, low, high):
    return pl.pallas_call(
        edge_kernel,
        in_specs=[SMEM, VMEM, VMEM, VMEM],
        out_specs=VMEM,
        out_shape=jax.ShapeDtypeStruct((4 * PAD, LANES), F32),
        compiler_params=params(16),
        name="ocean_edge",
    )(edge, ocean, low, high)


def early_kernel(
    edge_ref, atm_levels_ref, ocean_levels_ref, atm_ref, low_ref, high_ref,
    out_ref, surface_ref, own_out, halo_out, sea_out,
    levels, own, halo, sea, few, *rest,
):
    x_ref, x_sems = rest[:2]
    arrivals = fetch_atmos(0, atm_ref, x_ref, x_sems)
    levels[...] = jnp.zeros_like(levels)
    levels[0, 0:16, 0:16] = atm_levels_ref[...]
    levels[1, 0:16, 0:16] = ocean_levels_ref[...]
    write_operators(edge_ref, (levels[0], levels[1]), own, halo, sea)
    keep = fetch([(own, own_out), (halo, halo_out), (sea, sea_out)], few)
    sent = atmos_steps(
        0, arrivals, x_ref, low_ref, high_ref, own, halo, out_ref, surface_ref, *rest[2:]
    )
    for copy in keep + sent:
        copy.wait()


def early(edge, atm_levels, ocean_levels, atm, low, high, chunks=4):
    return pl.pallas_call(
        early_kernel,
        in_specs=[SMEM, VMEM, VMEM, HBM, VMEM, VMEM],
        out_specs=[HBM, VMEM, HBM, HBM, HBM],
        out_shape=[
            pltpu.HBM(atm.shape, F32),
            jax.ShapeDtypeStruct((16, WIDE), F32),
            pltpu.HBM(OWN, BF16),
            pltpu.HBM(FAR, BF16),
            pltpu.HBM(SEA, BF16),
        ],
        scratch_shapes=[
            pltpu.VMEM((2, LANES, LANES), F32),
            pltpu.VMEM(OWN, BF16),
            pltpu.VMEM(FAR, BF16),
            pltpu.VMEM(SEA, BF16),
            pltpu.SemaphoreType.DMA((3,)),
        ]
        + atmos_scratch(chunks),
        compiler_params=params(40),
        cost_estimate=cost(3 * 512 * 1024 * WIDE, 6),
        name="atmosphere_0",
    )(edge, atm_levels, ocean_levels, atm, low, high)


def ocean_steps(first, ocean_ref, low_ref, high_ref, side_ref, g_ref, flux_ref, out_ref, w):
    wide = ocean_ref.shape[2]

    def extend(rows, side):
        empty = jnp.zeros_like(side)
        before, after = jnp.where(first, empty, side), jnp.where(first, side, empty)
        return jnp.concatenate([before, rows, after], axis=0)

    halos = []
    for n, ref in enumerate((low_ref, high_ref)):
        side = side_ref[(2 + n) * PAD : (3 + n) * PAD]
        halos.append(extend(ref[WIDE : WIDE + wide].astype(F32), side).astype(BF16))
    for v in range(2):
        own = jnp.concatenate([ocean_ref[v, :, :LANES].T, ocean_ref[v, :, LANES:].T], axis=0)
        state = extend(own, side_ref[v * PAD : (v + 1) * PAD])
        high, low = split(state)
        left = jnp.concatenate([high, low, high] + halos, axis=1)
        g = g_ref[...]
        right = jnp.concatenate([g[:256], g[128:256], halo_rows(g[256:], v)], axis=0)
        for s in range(STEPS):
            w[s] = mxu(left, right[:, s * LANES : (s + 1) * LANES])
        w[STEPS] = state * diffuse**STEPS
        end = wide + PAD
        for s in range(1, STEPS + 1):
            w[s, 0:PAD] = jnp.where(first, mirror_low(w[s, PAD : 2 * PAD]), w[s, 0:PAD])
            w[s, end : end + PAD] = jnp.where(
                first, w[s, end : end + PAD], mirror_high(w[s, end - PAD : end])
            )
        for c in range(wide // LANES):
            at = PAD + c * LANES
            total = w[0, at : at + LANES]
            for s in range(1, STEPS + 1):
                total += w[s, at - s : at - s + LANES]
                total += w[s, at + s : at + s + LANES]
            final = total.T
            lanes = slice(c * LANES, (c + 1) * LANES)
            out_ref[v, :, lanes] = final
            out_ref[v, 0:8, lanes] = final[0:8] + couple * flux_ref[v, :, lanes]


def late_kernel(
    edge_ref, atm_ref, ocean_ref, low_ref, high_ref, side_ref, flux_ref, own_ref, halo_ref,
    sea_ref, _, out_ref, surface_ref, ocean_out, state, sea, own, halo, sea_w, few, *rest,
):
    x_ref, x_sems = rest[:2]
    arrivals = fetch(
        [(ocean_ref, state), (sea_ref, sea), (own_ref, own), (halo_ref, halo)], few
    )
    x_arrivals = fetch_atmos(1, atm_ref, x_ref, x_sems)
    for copy in arrivals:
        copy.wait()
    ocean_steps(
        edge_ref[0] == 0, state, low_ref, high_ref, side_ref, sea, flux_ref, ocean_out, sea_w
    )
    sent = atmos_steps(
        1, x_arrivals, x_ref, low_ref, high_ref, own, halo, out_ref, surface_ref, *rest[2:]
    )
    for copy in sent:
        copy.wait()


def late(edge, atm, ocean, low, high, side, flux, own, halo, sea, half, chunks=4):
    return pl.pallas_call(
        late_kernel,
        in_specs=[SMEM, HBM, HBM, VMEM, VMEM, VMEM, VMEM] + [HBM] * 4,
        out_specs=[HBM, VMEM, VMEM],
        out_shape=[
            pltpu.HBM(atm.shape, F32),
            jax.ShapeDtypeStruct((16, WIDE), F32),
            jax.ShapeDtypeStruct(ocean.shape, F32),
        ],
        scratch_shapes=[
            pltpu.VMEM(ocean.shape, F32),
            pltpu.VMEM(SEA, BF16),
            pltpu.VMEM(OWN, BF16),
            pltpu.VMEM(FAR, BF16),
            pltpu.VMEM((STEPS + 1, ocean.shape[2] + 2 * PAD, LANES), F32),
            pltpu.SemaphoreType.DMA((4,)),
        ]
        + atmos_scratch(chunks),
        input_output_aliases={10: 0},
        compiler_params=params(40),
        cost_estimate=cost(3 * 512 * 1024 * WIDE, 6),
        name="atmosphere_1",
    )(edge, atm, ocean, low, high, side, flux, own, halo, sea, half)


def masked(pair, i):
    return jnp.where(iota(pair.shape, 0) % GROUP == i, pair, 0.0)


def send_rows(states, start, next_ref, prev_ref):
    for offset, out_ref in ((-HALO, next_ref), (0, prev_ref)):
        both = jnp.concatenate([select_rows(state, offset) for state in states], axis=0)
        for c in range(both.shape[1] // LANES):
            chunk = both[:, c * LANES : (c + 1) * LANES].T.astype(BF16)
            out_ref[start + c * LANES : start + (c + 1) * LANES] = chunk


def pack_kernel(
    atm_ref, ocean_ref, next_ref, prev_ref, level_ref, x_ref, sea_state, few, sems
):
    chunks = sems.shape[0]
    width = WIDE // chunks
    cells = [pl.ds(n * width, width) for n in range(chunks)]
    copies = fetch([(atm_ref.at[:, :, c], x_ref.at[:, :, c]) for c in cells], sems)
    (arrival,) = fetch([(ocean_ref, sea_state)], few)
    arrival.wait()
    send_rows([sea_state[v].astype(BF16) for v in range(2)], WIDE, next_ref, prev_ref)
    for n, copy in enumerate(copies):
        copy.wait()
        lanes = slice(n * width, (n + 1) * width)
        states = [x_ref[v, :, lanes].astype(BF16) for v in range(2)]
        send_rows(states, n * width, next_ref, prev_ref)
        level_ref[:, :, lanes] = x_ref[:, 0:16, lanes]


def pack(atm, ocean, chunks=4):
    rows = jax.ShapeDtypeStruct((WIDE + ocean.shape[2], LANES), BF16)
    return pl.pallas_call(
        pack_kernel,
        in_specs=[HBM, HBM],
        out_specs=[VMEM] * 3,
        out_shape=[rows, rows, jax.ShapeDtypeStruct((2, 16, WIDE), F32)],
        scratch_shapes=[
            pltpu.VMEM(atm.shape, F32),
            pltpu.VMEM(ocean.shape, F32),
            pltpu.SemaphoreType.DMA((1,)),
            pltpu.SemaphoreType.DMA((chunks,)),
        ],
        compiler_params=params(24),
        cost_estimate=cost(1 << 28, 5),
        name="pack_halo",
    )(atm, ocean)


def forward_kernel(
    count_ref, owner_ref, block_ref, source_ref, level_ref, w_ref, out_ref, place_ref,
    tiles_ref, picked, contrib, left, sems,
):
    tiles = owner_ref.shape[1]
    per_row = WIDE // LANES
    size = tiles // sems.shape[0]
    some = [pl.ds(n * size, size) for n in range(sems.shape[0])]
    copies = fetch([(w_ref.at[t], tiles_ref.at[t]) for t in some], sems)

    source = source_ref[...]
    cell = (source & (per_row - 1)) * 16 + (source >> (per_row.bit_length() - 1))
    gather = onehot(iota((tiles, 256), 1).astype(F32) == column(cell.astype(F32)))
    for v in range(2):
        rounded = level_ref[v].astype(BF16)
        blocks = [rounded[:, b * LANES : (b + 1) * LANES] for b in range(per_row)]
        picked[v] = mxu(gather, jnp.concatenate(blocks, axis=0))
    owner = owner_ref[...].astype(F32)
    earlier = (column(owner) == owner) & (iota((tiles, tiles), 0) < iota((tiles, tiles), 1))
    rank = jnp.sum(jnp.where(earlier, 1.0, 0.0), axis=0, keepdims=True)
    live = iota((1, tiles), 1) < count_ref[0]
    place = jnp.where(live, owner_ref[...] * ROWS + rank.astype(jnp.int32), -64)
    index = jnp.where(live, owner_ref[...] * ROWS + 2 * CAP, -64)
    place_ref[0:1] = place
    place_ref[1:2] = jnp.where(live, cell, -64)
    place_ref[2:8] = jnp.zeros((6, tiles), jnp.int32)
    block = block_ref[...]
    lane = column(rank * 16.0 + ((block & 1) * 8 + (block >> 1)).astype(F32))
    names = onehot(iota((tiles, LANES), 1).astype(F32) == lane)
    part = out_ref.shape[0] // len(copies)

    for n, copy in enumerate(copies):
        copy.wait()
        row = iota((part, tiles), 0) + n * part
        here = slice(n * part, (n + 1) * part)
        for m, at in enumerate((place, place + CAP, index)):
            left[here, m * tiles : (m + 1) * tiles] = onehot(row == at)
        for t in range(n * size, (n + 1) * size, GROUP):
            rows = slice(t, t + GROUP)
            pair = jnp.concatenate([picked[0, rows], picked[1, rows]], axis=0)
            spread = jnp.concatenate([masked(pair, i).astype(BF16) for i in range(GROUP)], axis=1)
            both = mxu(spread, tiles_ref[rows].reshape(GROUP * LANES, LANES))
            contrib[0, rows] = both[:GROUP]
            contrib[1, rows] = both[GROUP:]

    first = jnp.concatenate(split(contrib[0]), axis=1)
    second = jnp.concatenate(split(contrib[1]), axis=1)
    third = jnp.concatenate([names, jnp.zeros_like(names)], axis=1)
    out = mxu(left[...], jnp.concatenate([first, second, third], axis=0))
    out_ref[...] = out[:, :LANES] + out[:, LANES:]


def forward(count, owner, block, source, level, weights, devices, parts=8):
    tiles = weights.shape[0]
    return pl.pallas_call(
        forward_kernel,
        in_specs=[SMEM, VMEM, VMEM, VMEM, VMEM, HBM],
        out_specs=[VMEM] * 2,
        out_shape=[
            jax.ShapeDtypeStruct((devices * ROWS, LANES), F32),
            jax.ShapeDtypeStruct((8, tiles), jnp.int32),
        ],
        scratch_shapes=[
            pltpu.VMEM(weights.shape, BF16),
            pltpu.VMEM((2, tiles, LANES), F32),
            pltpu.VMEM((2, tiles, LANES), F32),
            pltpu.VMEM((devices * ROWS, 3 * tiles), BF16),
            pltpu.SemaphoreType.DMA((parts,)),
        ],
        compiler_params=params(32),
        cost_estimate=cost(32 * tiles * LANES * LANES, 9),
        name="tiles_forward",
    )(count, owner, block, source, level, weights)


def combine_kernel(inbox_ref, ocean_ref, out_ref, flux_ref):
    devices = inbox_ref.shape[0] // ROWS

    def plane(r):
        return pl.ds(r, devices, stride=ROWS)

    names = inbox_ref[plane(6), :]
    parts = []
    for r in range(2 * CAP):
        value = inbox_ref[plane(r), :]
        high, low = split(value)
        rest = (value - high.astype(F32) - low.astype(F32)).astype(BF16)
        parts += [high, low, rest]
    summed = mxu(names.T.astype(BF16), jnp.concatenate(parts, axis=1))
    fields = []
    for v in range(2):
        received = 0.0
        for k in range(CAP):
            rows = summed[k * 16 : (k + 1) * 16]
            for term in range(3):
                at = ((v * CAP + k) * 3 + term) * LANES
                received = received + rows[:, at : at + LANES]
        surface = ocean_ref[v, 0:8]
        flux = received - jnp.concatenate([surface[:, :LANES], surface[:, LANES:]], axis=0)
        flux_ref[v] = jnp.concatenate([flux[:8], flux[8:]], axis=1)
        sent = flux.astype(BF16).astype(F32)
        empty = jnp.zeros_like(sent)
        for k in range(CAP):
            stack = [sent if j == k else empty for j in range(8)]
            fields.append(jnp.concatenate(stack, axis=0).astype(BF16))
    outgoing = mxu(names.astype(BF16), jnp.concatenate(fields, axis=1))
    for r in range(2 * CAP):
        out_ref[plane(r), :] = outgoing[:, r * LANES : (r + 1) * LANES]
    for r in range(2 * CAP, ROWS):
        out_ref[plane(r), :] = jnp.zeros((devices, LANES), F32)


def combine(inbox, ocean):
    return pl.pallas_call(
        combine_kernel,
        in_specs=[VMEM, VMEM],
        out_specs=[VMEM, VMEM],
        out_shape=[
            jax.ShapeDtypeStruct(inbox.shape, F32),
            jax.ShapeDtypeStruct((2, 8, 256), F32),
        ],
        compiler_params=params(24),
        name="ocean_flux",
    )(inbox, ocean)


def backward_kernel(
    place_ref, inbox_ref, w_ref, zero_ref, one_ref, _, out_ref,
    tiles_ref, picked, terms, held, sems, parts,
):
    tiles = place_ref.shape[1]
    size = tiles // parts.shape[0]
    some = [pl.ds(n * size, size) for n in range(parts.shape[0])]
    arrivals = fetch([(w_ref.at[t], tiles_ref.at[t]) for t in some], parts)
    per_row = WIDE // LANES
    place = column(place_ref[0:1].astype(F32)).astype(jnp.int32)
    inbox = inbox_ref[...].astype(BF16)
    slot = iota((tiles, inbox.shape[0]), 1)
    for v in range(2):
        picked[v] = mxu(onehot(slot == place + v * CAP), inbox)
    scatter = onehot(iota((256, tiles), 0) == place_ref[1:2])

    for t in range(0, tiles, GROUP):
        if t % size == 0:
            arrivals[t // size].wait()
        rows = slice(t, t + GROUP)
        pair = jnp.concatenate([picked[0, rows], picked[1, rows]], axis=0)
        weights = tiles_ref[rows].reshape(GROUP * LANES, LANES)
        wide = mxu(pair.astype(BF16), weights, ((1,), (1,)))
        both = 0.0
        for i in range(GROUP):
            both = both + masked(wide[:, i * LANES : (i + 1) * LANES], i)
        terms[0, rows] = both[:GROUP]
        terms[1, rows] = both[GROUP:]

    halves = [part for v in range(2) for part in split(terms[v])]
    summed = mxu(scatter, jnp.concatenate(halves, axis=1))
    copies = []
    for v, level_ref in enumerate((zero_ref, one_ref)):
        at = 2 * v * LANES
        returned = summed[:, at : at + LANES] + summed[:, at + LANES : at + 2 * LANES]
        for b in range(per_row):
            lanes = slice(b * LANES, (b + 1) * LANES)
            held[v, :, lanes] = level_ref[:, lanes] - couple * returned[b * 16 : (b + 1) * 16]
        copy = pltpu.make_async_copy(held.at[v], out_ref.at[v, pl.ds(0, 16)], sems.at[v])
        copy.start()
        copies.append(copy)
    for copy in copies:
        copy.wait()


def backward(place, inbox, weights, zero, one, atm, parts=8):
    tiles = weights.shape[0]
    return pl.pallas_call(
        backward_kernel,
        in_specs=[VMEM, VMEM, HBM, VMEM, VMEM, HBM],
        out_specs=HBM,
        out_shape=pltpu.HBM(atm.shape, F32),
        scratch_shapes=[
            pltpu.VMEM(weights.shape, BF16),
            pltpu.VMEM((2, tiles, LANES), F32),
            pltpu.VMEM((2, tiles, LANES), F32),
            pltpu.VMEM((2, 16, WIDE), F32),
            pltpu.SemaphoreType.DMA((2,)),
            pltpu.SemaphoreType.DMA((parts,)),
        ],
        input_output_aliases={5: 0},
        compiler_params=params(32),
        cost_estimate=cost(32 * tiles * LANES * LANES, 1),
        name="tiles_backward",
    )(place, inbox, weights, zero, one, atm)


def swap(rows):
    devices = lax.axis_size(RING)
    boxes = rows.reshape(devices, ROWS, LANES)
    return lax.all_to_all(boxes, RING, split_axis=0, concat_axis=0, tiled=True).reshape(rows.shape)


def per_device(
    atm_state,
    ocean_state,
    atm_levels,
    ocean_levels,
    tile_weight,
    tile_owner,
    tile_block,
    tile_source,
    tile_count,
):
    devices = lax.axis_size(RING)
    tiles = tile_weight.shape[0]
    atm = atm_state.reshape(2, 256, WIDE)
    ocean = ocean_state.reshape(2, 128, 256)
    grp, dom = lax.axis_index("grp"), lax.axis_index("dom")
    last = lax.axis_size("dom") - 1
    edge = jnp.stack([grp, (dom == 0).astype(jnp.int32), (dom == last).astype(jnp.int32)])

    atm = pltpu.with_memory_space_constraint(atm, pltpu.HBM)
    sea_state = pltpu.with_memory_space_constraint(ocean, pltpu.HBM)
    tile_weight = pltpu.with_memory_space_constraint(tile_weight, pltpu.HBM)
    lists = [x.reshape(1, tiles) for x in (tile_owner, tile_block, tile_source)]
    to_next, to_prev, level = pack(atm, sea_state)
    forth = [(i, (i + 1) % devices) for i in range(devices)]
    back = [(target, source) for source, target in forth]
    low = lax.ppermute(to_next, RING, forth)
    high = lax.ppermute(to_prev, RING, back)
    outbox, place = forward(tile_count, *lists, level, tile_weight, devices)
    inbox = swap(outbox)
    columns = edge_rows(edge, ocean, low, high)
    side = lax.ppermute(columns, "grp", [(0, 1), (1, 0)])
    half, zero, *operators = early(edge, atm_levels, ocean_levels, atm, low, high)
    operators = [pltpu.with_memory_space_constraint(x, pltpu.HBM) for x in operators]
    inbox, half, side = lax.optimization_barrier((inbox, half, side))
    outgoing, flux = combine(inbox, ocean)
    returned = swap(outgoing)
    whole, one, ocean_final = late(
        edge, atm, sea_state, low, high, side, flux, *operators, half
    )
    returned, whole, ocean_final = lax.optimization_barrier((returned, whole, ocean_final))
    atm_final = backward(place, returned, tile_weight, zero, one, whole)
    return atm_final.reshape(atm_state.shape), ocean_final.reshape(ocean_state.shape)


def solution(mesh):
    in_specs = (
        P(None, None, RING, None),
        P(None, None, "dom", "grp"),
        P(),
        P(),
        P(RING, None, None),
        P(RING, None),
        P(RING),
        P(RING),
        P(RING),
    )
    out_specs = (P(None, None, RING, None), P(None, None, "dom", "grp"))
    return jax.shard_map(
        per_device, mesh=mesh, in_specs=in_specs, out_specs=out_specs, check_vma=False
    )
```

```python
import functools
import math

import jax
import jax.numpy as jnp
from jax import lax
from jax.experimental import pallas as pl
from jax.experimental.pallas import tpu as pltpu
from jax.sharding import PartitionSpec as P

STEPS = 4
HALO = STEPS
CAP = 3
ROWS = 8
LANES = 128
GROUP = 8
PAD = 8
AHEAD = 64
WIDE = 2048
RING = ("grp", "dom")
F32 = jnp.float32
BF16 = jnp.bfloat16

diffuse = 0.2
vertical = 0.25
couple = 0.5
MIB = 1 << 20


VMEM = pl.BlockSpec(memory_space=pltpu.VMEM)
HBM = pl.BlockSpec(memory_space=pltpu.HBM)
SMEM = pl.BlockSpec(memory_space=pltpu.SMEM)


def params(mib):
    return pltpu.CompilerParams(vmem_limit_bytes=mib * MIB)


def cost(flops, mib):
    return pl.CostEstimate(flops=flops, bytes_accessed=mib * MIB, transcendentals=0)


def fetch(pairs, sems):
    copies = []
    for n, (source, target) in enumerate(pairs):
        copies.append(pltpu.make_async_copy(source, target, sems.at[n]))
        copies[-1].start()
    return copies


def iota(shape, dim):
    return lax.broadcasted_iota(jnp.int32, shape, dim)


def onehot(mask):
    return jnp.where(mask, 1.0, 0.0).astype(BF16)


def split(value):
    high = value.astype(BF16)
    return high, (value - high.astype(F32)).astype(BF16)


def mxu(left, right, dims=((1,), (0,))):
    return lax.dot_general(left, right, (dims, ((), ())), preferred_element_type=F32)


def exact(left, right):
    return lax.dot_general(
        left, right, (((1,), (0,)), ((), ())), precision=lax.Precision.HIGHEST,
        preferred_element_type=F32,
    )


def column(row):
    n = row.shape[1]
    eye = iota((n, n), 0) == iota((n, n), 1)
    return jnp.sum(jnp.where(eye, jnp.broadcast_to(row, (n, n)), 0.0), axis=1, keepdims=True)


def select_rows(state):
    rows = state.shape[0]
    deep = rows // 16
    out, col = iota((32 * HALO, rows), 0), iota((32 * HALO, rows), 1)
    first = ((out >> 2) & 15) * deep + (out & 3)
    return mxu(onehot(col == jnp.where(out < 16 * HALO, first + deep - HALO, first)), state)


def coefficients():
    table = []
    for s in range(STEPS):
        by_level = []
        for i in range(STEPS - s + 1):
            by_distance = [0.0] * (STEPS + 1)
            for k in range(s, STEPS - i + 1, 2):
                q = STEPS - k - i
                trinomial = [1]
                for _ in range(q):
                    padded = [0, 0] + trinomial + [0, 0]
                    trinomial = [sum(padded[j : j + 3]) for j in range(len(trinomial) + 2)]
                scale = math.comb(k, (k - s) // 2) * math.comb(STEPS, k)
                scale *= math.comb(STEPS - k, i) * diffuse ** (k + q)
                for d in range(q + 1):
                    by_distance[d] += scale * trinomial[q + d]
            by_level.append(by_distance)
        table.append(by_level)
    return table


def lookup(weights, distance):
    total = 0.0
    for d, weight in enumerate(weights):
        if weight:
            total = jnp.where(distance == d, weight, total)
    return total


def stencils(own, image):
    table = coefficients()
    x = iota((16, LANES), 1) & (own - 1)
    r = iota((16, LANES), 0)
    sources = [(r & (own - 1), own), ((r & 3) - HALO, HALO), ((r & 3) + own, HALO)]
    result = [[[] for _ in by_level] for by_level in table]
    for xs, depth in sources:
        distance = jnp.abs(xs - x)
        if image is not None:
            first, last = image
            below = jnp.where(first == 1, jnp.abs(xs + x + 2), STEPS + 1)
            above = jnp.where(last == 1, jnp.abs(2 * own - xs - x), STEPS + 1)
            inside = ((first == 0) | (xs >= 0)) & ((last == 0) | (xs < own))
        for s, by_level in enumerate(table):
            for i, weights in enumerate(by_level):
                part = lookup(weights, distance)
                if image is not None:
                    part = part - lookup(weights, below) - lookup(weights, above)
                    part = jnp.where(inside, part, 0.0)
                result[s][i] += [part] * depth
    return [[jnp.concatenate(parts, axis=0) for parts in by_level] for by_level in result]


def small_product(left, right):
    total = 0.0
    for k in range(16):
        total = total + left[:, k : k + 1] * right[k : k + 1, :]
    return total


def operators(levels, own, image):
    rows, cols = 16 * own + 32 * HALO, 16 * own
    shift = own.bit_length() - 1
    one = vertical * levels.T[:16]
    two = small_product(one, one)
    stack = [half for p in (one, two, small_product(two, one), small_product(two, two))
             for half in split(p)]
    stack = jnp.concatenate([half.astype(F32) for half in stack], axis=0).astype(BF16)
    spread = onehot(iota((LANES, cols), 0) == (iota((LANES, cols), 1) >> shift))
    wide = mxu(stack, spread).astype(BF16)
    r, c = iota((rows, LANES), 0), iota((rows, LANES), 1)
    level = jnp.where(r < cols, r >> shift, (r >> 2) & 15)
    mixed = [mxu(onehot(((c & 15) == level) & ((c >> 5) == i)), wide) for i in range(STEPS)]
    r, c = iota((rows, cols), 0), iota((rows, cols), 1)
    same = jnp.where(r < cols, r >> shift, (r >> 2) & 15) == (c >> shift)
    result = []
    for by_level in stencils(own, image):
        total = 0.0
        for i, part in enumerate(by_level):
            part = jnp.concatenate([part] * (cols // LANES), axis=1)
            total = total + (jnp.where(same, part, 0.0) if i == 0 else part * mixed[i - 1])
        result.append(total)
    return result


def write_atmos(levels, own_ref, halo_ref):
    for s, part in enumerate(operators(levels, 16, None)):
        high, low = split(part[:256])
        lanes = slice((s & 1) * 256, (s & 1) * 256 + 256)
        if s < 2:
            own_ref[0:256, lanes] = low
            own_ref[256:512, lanes] = high
        else:
            own_ref[512:768, lanes] = high
        halo_ref[:, s * 256 : (s + 1) * 256] = part[256:].astype(BF16)


def write_ocean(edge_ref, levels, ocean_ref):
    image = (edge_ref[1], edge_ref[2])
    for s, part in enumerate(operators(levels, 8, image)):
        lanes = slice(s * LANES, (s + 1) * LANES)
        high, low = split(part[:128])
        ocean_ref[0:128, lanes] = low
        ocean_ref[128:256, lanes] = high
        ocean_ref[256:384, lanes] = part[128:].astype(BF16)


OWN, FAR, SEA = (768, 512), (128, 1024), (384, 512)


def mirror_low(rows):
    r = iota(rows.shape, 0)
    total = jnp.zeros_like(rows)
    for j in range(3):
        total = jnp.where(r == 6 - j, -rows[j : j + 1], total)
    return total


def mirror_high(rows):
    r = iota(rows.shape, 0)
    total = jnp.zeros_like(rows)
    for j in range(3):
        total = jnp.where(r == 1 + j, -rows[7 - j : 8 - j], total)
    return total


def halo_rows(halo, v):
    half = 16 * HALO
    empty = jnp.zeros((half, halo.shape[1]), halo.dtype)
    blocks = []
    for side in range(2):
        part = halo[side * half : (side + 1) * half]
        blocks += [part, empty] if v == 0 else [empty, part]
    return jnp.concatenate(blocks, axis=0)


def atmos_steps(v, arrivals, x_ref, low_ref, high_ref, own_ref, halo_ref, out_ref, surface_ref,
                left, main, minor, w, held, sems):
    chunks = len(arrivals)
    size = WIDE // chunks
    main[0:512] = own_ref[0:512]
    main[512:768] = own_ref[256:512]
    main[768:1024] = halo_rows(halo_ref[:, 0:512], v)
    minor[0:256] = own_ref[512:768]
    minor[256:512] = halo_rows(halo_ref[:, 512:1024], v)
    copies = []
    for n in range(chunks + 1):
        if n < chunks:
            arrivals[n].wait()
            start = n * size
            for c in range(size // LANES):
                rows = slice(c * LANES, (c + 1) * LANES)
                at = start + c * LANES
                for h in range(2):
                    state = x_ref[h * LANES : (h + 1) * LANES, at : at + LANES].T
                    high, low = split(state)
                    lanes = slice(h * LANES, (h + 1) * LANES)
                    w[STEPS, PAD + at : PAD + at + LANES, lanes] = state * diffuse**STEPS
                    left[rows, h * LANES : (h + 1) * LANES] = high
                    left[rows, 256 + h * LANES : 256 + (h + 1) * LANES] = low
                    left[rows, 512 + h * LANES : 512 + (h + 1) * LANES] = high
            left[:, 768:896] = low_ref[start : start + size]
            left[:, 896:1024] = high_ref[start : start + size]
            rows = slice(PAD + start, PAD + start + size)
            for s in range(2):
                lanes = slice(s * 256, (s + 1) * 256)
                w[s, rows] = mxu(left[...], main[:, lanes])
                w[2 + s, rows] = mxu(left[:, 512:1024], minor[:, lanes])
        if n == 0:
            for s in range(1, STEPS + 1):
                w[s, 0:PAD] = mirror_low(w[s, PAD : 2 * PAD])
        if n == chunks - 1:
            for s in range(1, STEPS + 1):
                w[s, WIDE + PAD : WIDE + 2 * PAD] = mirror_high(w[s, WIDE : WIDE + PAD])
        if n > 0:
            start = (n - 1) * size
            for c in range(size // LANES):
                at = PAD + start + c * LANES
                for h in range(2):
                    lanes = slice(h * LANES, (h + 1) * LANES)
                    total = w[0, at : at + LANES, lanes]
                    for s in range(1, STEPS + 1):
                        total += w[s, at - s : at - s + LANES, lanes]
                        total += w[s, at + s : at + s + LANES, lanes]
                    held[lanes, at - PAD : at - PAD + LANES] = total.T
            cells = pl.ds(start, size)
            surface_ref[:, start : start + size] = held[0:16, start : start + size]
            copy = pltpu.make_async_copy(
                held.at[:, cells], out_ref.at[v, :, cells], sems.at[n - 1]
            )
            copy.start()
            copies.append(copy)
    return copies


def atmos_scratch(chunks):
    size = WIDE // chunks
    return [
        pltpu.VMEM((256, WIDE), F32),
        pltpu.SemaphoreType.DMA((chunks,)),
        pltpu.VMEM((size, 1024), BF16),
        pltpu.VMEM((1024, 512), BF16),
        pltpu.VMEM((512, 512), BF16),
        pltpu.VMEM((STEPS + 1, WIDE + 2 * PAD, 256), F32),
        pltpu.VMEM((256, WIDE), F32),
        pltpu.SemaphoreType.DMA((chunks,)),
    ]


def fetch_atmos(v, atm_ref, x_ref, sems):
    size = WIDE // sems.shape[0]
    cells = [pl.ds(n * size, size) for n in range(sems.shape[0])]
    copies = [
        pltpu.make_async_copy(atm_ref.at[v, :, c], x_ref.at[:, c], sems.at[n])
        for n, c in enumerate(cells)
    ]
    copies[0].start()
    return copies


def edge_kernel(edge_ref, ocean_ref, low_ref, high_ref, out_ref):
    first = edge_ref[0] == 0
    for v in range(2):
        before, after = ocean_ref[v, :, 0:LANES].T[:PAD], ocean_ref[v, :, LANES:].T[LANES - PAD :]
        out_ref[v * PAD : (v + 1) * PAD] = jnp.where(first, after, before)
    for n, ref in enumerate((low_ref, high_ref)):
        before, after = ref[WIDE : WIDE + 16], ref[WIDE + 240 : WIDE + 256]
        edge = jnp.where(first, after.astype(F32)[16 - PAD :], before.astype(F32)[:PAD])
        out_ref[(2 + n) * PAD : (3 + n) * PAD] = edge


def edge_rows(edge, ocean, low, high):
    return pl.pallas_call(
        edge_kernel,
        in_specs=[SMEM, VMEM, VMEM, VMEM],
        out_specs=VMEM,
        out_shape=jax.ShapeDtypeStruct((4 * PAD, LANES), F32),
        compiler_params=params(16),
        name="ocean_edge",
    )(edge, ocean, low, high)


def early_kernel(
    edge_ref, atm_levels_ref, ocean_levels_ref, atm_ref, low_ref, high_ref,
    out_ref, surface_ref, halo, sea, own_out, levels, own, few, *rest,
):
    x_ref, x_sems = rest[:2]
    arrivals = fetch_atmos(0, atm_ref, x_ref, x_sems)
    levels[...] = jnp.zeros_like(levels)
    levels[0, 0:16, 0:16] = atm_levels_ref[...]
    levels[1, 0:16, 0:16] = ocean_levels_ref[...]
    write_atmos(levels[0], own, halo)
    for copy in arrivals[1:]:
        copy.start()
    keep = fetch([(own, own_out)], few)
    sent = atmos_steps(
        0, arrivals, x_ref, low_ref, high_ref, own, halo, out_ref, surface_ref, *rest[2:]
    )
    write_ocean(edge_ref, levels[1], sea)
    for copy in keep + sent:
        copy.wait()


def early(edge, atm_levels, ocean_levels, atm, low, high, chunks=4):
    return pl.pallas_call(
        early_kernel,
        in_specs=[SMEM, VMEM, VMEM, HBM, VMEM, VMEM],
        out_specs=[HBM, VMEM, VMEM, VMEM, HBM],
        out_shape=[
            pltpu.HBM(atm.shape, F32),
            jax.ShapeDtypeStruct((16, WIDE), F32),
            jax.ShapeDtypeStruct(FAR, BF16),
            jax.ShapeDtypeStruct(SEA, BF16),
            pltpu.HBM(OWN, BF16),
        ],
        scratch_shapes=[
            pltpu.VMEM((2, LANES, LANES), F32),
            pltpu.VMEM(OWN, BF16),
            pltpu.SemaphoreType.DMA((1,)),
        ]
        + atmos_scratch(chunks),
        compiler_params=params(40),
        cost_estimate=cost(3 * 512 * 1024 * WIDE, 6),
        name="atmosphere_0",
    )(edge, atm_levels, ocean_levels, atm, low, high)


def ocean_steps(v, first, ocean_ref, low_ref, high_ref, side_ref, g_ref, flux_ref, out_ref, w):
    wide = ocean_ref.shape[2]

    def extend(rows, side):
        empty = jnp.zeros_like(side)
        before, after = jnp.where(first, empty, side), jnp.where(first, side, empty)
        return jnp.concatenate([before, rows, after], axis=0)

    halos = []
    for n, ref in enumerate((low_ref, high_ref)):
        side = side_ref[(2 + n) * PAD : (3 + n) * PAD]
        halos.append(extend(ref[WIDE : WIDE + wide].astype(F32), side).astype(BF16))
    own = jnp.concatenate([ocean_ref[v, :, :LANES].T, ocean_ref[v, :, LANES:].T], axis=0)
    state = extend(own, side_ref[v * PAD : (v + 1) * PAD])
    high, low = split(state)
    left = jnp.concatenate([high, low, high] + halos, axis=1)
    g = g_ref[...]
    right = jnp.concatenate([g[:256], g[128:256], halo_rows(g[256:], v)], axis=0)
    for s in range(0, STEPS, 2):
        both = mxu(left, right[:, s * LANES : (s + 2) * LANES])
        w[s], w[s + 1] = both[:, :LANES], both[:, LANES:]
    w[STEPS] = state * diffuse**STEPS
    end = wide + PAD
    for s in range(1, STEPS + 1):
        w[s, 0:PAD] = jnp.where(first, mirror_low(w[s, PAD : 2 * PAD]), w[s, 0:PAD])
        w[s, end : end + PAD] = jnp.where(
            first, w[s, end : end + PAD], mirror_high(w[s, end - PAD : end])
        )
    for c in range(wide // LANES):
        at = PAD + c * LANES
        total = w[0, at : at + LANES]
        for s in range(1, STEPS + 1):
            total += w[s, at - s : at - s + LANES]
            total += w[s, at + s : at + s + LANES]
        final = total.T
        lanes = slice(c * LANES, (c + 1) * LANES)
        out_ref[v, :, lanes] = final
        out_ref[v, 0:8, lanes] = final[0:8] + couple * flux_ref[v, :, lanes]


def late_kernel(
    edge_ref, atm_ref, ocean_ref, low_ref, high_ref, side_ref, flux_ref, halo_ref, sea_ref,
    own_ref, _, out_ref, surface_ref, ocean_out, own, sea_w, few, *rest,
):
    x_ref, x_sems = rest[:2]
    (arrival,) = fetch([(own_ref, own)], few)
    x_arrivals = fetch_atmos(1, atm_ref, x_ref, x_sems)
    ocean = (
        edge_ref[0] == 0, ocean_ref, low_ref, high_ref, side_ref, sea_ref, flux_ref, ocean_out,
        sea_w,
    )
    ocean_steps(0, *ocean)
    for copy in x_arrivals[1:]:
        copy.start()
    arrival.wait()
    sent = atmos_steps(
        1, x_arrivals, x_ref, low_ref, high_ref, own, halo_ref, out_ref, surface_ref, *rest[2:]
    )
    ocean_steps(1, *ocean)
    for copy in sent:
        copy.wait()


def late(edge, atm, ocean, low, high, side, flux, halo, sea, own, half, chunks=4):
    return pl.pallas_call(
        late_kernel,
        in_specs=[SMEM, HBM] + [VMEM] * 7 + [HBM] * 2,
        out_specs=[HBM, VMEM, VMEM],
        out_shape=[
            pltpu.HBM(atm.shape, F32),
            jax.ShapeDtypeStruct((16, WIDE), F32),
            jax.ShapeDtypeStruct(ocean.shape, F32),
        ],
        scratch_shapes=[
            pltpu.VMEM(OWN, BF16),
            pltpu.VMEM((STEPS + 1, ocean.shape[2] + 2 * PAD, LANES), F32),
            pltpu.SemaphoreType.DMA((1,)),
        ]
        + atmos_scratch(chunks),
        input_output_aliases={10: 0},
        compiler_params=params(40),
        cost_estimate=cost(3 * 512 * 1024 * WIDE, 6),
        name="atmosphere_1",
    )(edge, atm, ocean, low, high, side, flux, halo, sea, own, half)


def masked(pair, i):
    return jnp.where(iota(pair.shape, 0) % GROUP == i, pair, 0.0)


def send_rows(states, start, next_ref, prev_ref):
    picked = [select_rows(state) for state in states]
    half = 16 * HALO
    for rows, out_ref in ((slice(0, half), next_ref), (slice(half, None), prev_ref)):
        both = jnp.concatenate([part[rows] for part in picked], axis=0)
        for c in range(both.shape[1] // LANES):
            chunk = both[:, c * LANES : (c + 1) * LANES].T.astype(BF16)
            out_ref[start + c * LANES : start + (c + 1) * LANES] = chunk


def pack_kernel(
    atm_ref, ocean_ref, w_ref, next_ref, prev_ref, level_ref, ahead_ref, x_ref, sea_state, few, sems
):
    chunks = sems.shape[0]
    width = WIDE // chunks
    cells = [pl.ds(n * width, width) for n in range(chunks)]
    (arrival,) = fetch([(ocean_ref, sea_state)], few)
    copies = fetch([(atm_ref.at[:, :, c], x_ref.at[:, :, c]) for c in cells], sems)
    ahead = pltpu.make_async_copy(w_ref.at[pl.ds(0, AHEAD)], ahead_ref, few.at[1])
    ahead.start()
    arrival.wait()
    send_rows([sea_state[v].astype(BF16) for v in range(2)], WIDE, next_ref, prev_ref)
    for n, copy in enumerate(copies):
        copy.wait()
        lanes = slice(n * width, (n + 1) * width)
        states = [x_ref[v, :, lanes].astype(BF16) for v in range(2)]
        send_rows(states, n * width, next_ref, prev_ref)
        level_ref[:, :, lanes] = x_ref[:, 0:16, lanes]
    ahead.wait()


def pack(atm, ocean, weights, chunks=2):
    rows = jax.ShapeDtypeStruct((WIDE + ocean.shape[2], LANES), BF16)
    return pl.pallas_call(
        pack_kernel,
        in_specs=[HBM, HBM, HBM],
        out_specs=[VMEM] * 4,
        out_shape=[
            rows,
            rows,
            jax.ShapeDtypeStruct((2, 16, WIDE), F32),
            jax.ShapeDtypeStruct((AHEAD, LANES, LANES), BF16),
        ],
        scratch_shapes=[
            pltpu.VMEM(atm.shape, F32),
            pltpu.VMEM(ocean.shape, F32),
            pltpu.SemaphoreType.DMA((2,)),
            pltpu.SemaphoreType.DMA((chunks,)),
        ],
        compiler_params=params(24),
        cost_estimate=cost(1 << 28, 5),
        name="pack_halo",
    )(atm, ocean, weights)


def fetch_tiles(w_ref, tiles_ref, sems):
    count = tiles_ref.shape[0]
    first, size = w_ref.shape[0] - count, count // sems.shape[0]
    starts = [n * size for n in range(sems.shape[0])]
    return fetch(
        [(w_ref.at[pl.ds(first + t, size)], tiles_ref.at[pl.ds(t, size)]) for t in starts], sems
    )


def held_tiles(t, ahead_ref, tiles_ref, copies):
    ahead = 0 if ahead_ref is None else ahead_ref.shape[0]
    if t < ahead:
        held = ahead_ref[t : t + GROUP]
    else:
        size = tiles_ref.shape[0] // len(copies)
        if (t - ahead) % size == 0:
            copies[(t - ahead) // size].wait()
        held = tiles_ref[t - ahead : t - ahead + GROUP]
    return held.reshape(GROUP * LANES, LANES)


def forward_kernel(
    count_ref, owner_ref, block_ref, source_ref, level_ref, ahead_ref, w_ref, out_ref, place_ref,
    tiles_ref, picked, contrib, left, sems,
):
    tiles = owner_ref.shape[1]
    per_row = WIDE // LANES
    copies = fetch_tiles(w_ref, tiles_ref, sems)

    source = source_ref[...]
    cell = (source & (per_row - 1)) * 16 + (source >> (per_row.bit_length() - 1))
    gather = onehot(iota((tiles, 256), 1).astype(F32) == column(cell.astype(F32)))
    for v in range(2):
        rounded = level_ref[v].astype(BF16)
        blocks = [rounded[:, b * LANES : (b + 1) * LANES] for b in range(per_row)]
        picked[v] = mxu(gather, jnp.concatenate(blocks, axis=0))
    owner = owner_ref[...].astype(F32)
    earlier = (column(owner) == owner) & (iota((tiles, tiles), 0) < iota((tiles, tiles), 1))
    rank = jnp.sum(jnp.where(earlier, 1.0, 0.0), axis=0, keepdims=True)
    live = iota((1, tiles), 1) < count_ref[...]
    place = jnp.where(live, owner_ref[...] * ROWS + rank.astype(jnp.int32), -64)
    index = jnp.where(live, owner_ref[...] * ROWS + 2 * CAP, -64)
    place_ref[0:1] = place
    place_ref[1:2] = jnp.where(live, cell, -64)
    place_ref[2:8] = jnp.zeros((6, tiles), jnp.int32)
    block = block_ref[...]
    lane = column(rank * 16.0 + ((block & 1) * 8 + (block >> 1)).astype(F32))
    names = onehot(iota((tiles, LANES), 1).astype(F32) == lane)
    part = out_ref.shape[0] * GROUP // tiles

    for t in range(0, tiles, GROUP):
        held = held_tiles(t, ahead_ref, tiles_ref, copies)
        row = iota((part, tiles), 0) + t // GROUP * part
        here = slice(t // GROUP * part, (t // GROUP + 1) * part)
        for m, at in enumerate((place, place + CAP, index)):
            left[here, m * tiles : (m + 1) * tiles] = onehot(row == at)
        rows = slice(t, t + GROUP)
        pair = jnp.concatenate([picked[0, rows], picked[1, rows]], axis=0)
        spread = jnp.concatenate([masked(pair, i).astype(BF16) for i in range(GROUP)], axis=1)
        both = mxu(spread, held)
        contrib[0, rows] = both[:GROUP]
        contrib[1, rows] = both[GROUP:]

    first = jnp.concatenate(split(contrib[0]), axis=1)
    second = jnp.concatenate(split(contrib[1]), axis=1)
    third = jnp.concatenate([names, jnp.zeros_like(names)], axis=1)
    out = mxu(left[...], jnp.concatenate([first, second, third], axis=0))
    out_ref[...] = out[:, :LANES] + out[:, LANES:]


def forward(count, owner, block, source, level, ahead, weights, devices, parts=4):
    tiles = weights.shape[0]
    return pl.pallas_call(
        forward_kernel,
        in_specs=[VMEM] * 6 + [HBM],
        out_specs=[VMEM] * 2,
        out_shape=[
            jax.ShapeDtypeStruct((devices * ROWS, LANES), F32),
            jax.ShapeDtypeStruct((8, tiles), jnp.int32),
        ],
        scratch_shapes=[
            pltpu.VMEM((tiles - AHEAD, LANES, LANES), BF16),
            pltpu.VMEM((2, tiles, LANES), F32),
            pltpu.VMEM((2, tiles, LANES), F32),
            pltpu.VMEM((devices * ROWS, 3 * tiles), BF16),
            pltpu.SemaphoreType.DMA((parts,)),
        ],
        compiler_params=params(32),
        cost_estimate=cost(32 * tiles * LANES * LANES, 9),
        name="tiles_forward",
    )(count, owner, block, source, level, ahead, weights)


def combine_kernel(inbox_ref, ocean_ref, out_ref, flux_ref, boxes):
    devices = inbox_ref.shape[0] // ROWS

    def plane(r):
        return pl.ds(r, devices, stride=ROWS)

    names = inbox_ref[plane(6), :]
    parts = []
    for r in range(2 * CAP):
        value = inbox_ref[plane(r), :]
        high, low = split(value)
        rest = (value - high.astype(F32) - low.astype(F32)).astype(BF16)
        parts += [high, low, rest]
    summed = mxu(names.T.astype(BF16), jnp.concatenate(parts, axis=1))
    fields = []
    for v in range(2):
        received = 0.0
        for k in range(CAP):
            rows = summed[k * 16 : (k + 1) * 16]
            for term in range(3):
                at = ((v * CAP + k) * 3 + term) * LANES
                received = received + rows[:, at : at + LANES]
        surface = ocean_ref[v, 0:8]
        flux = received - jnp.concatenate([surface[:, :LANES], surface[:, LANES:]], axis=0)
        flux_ref[v] = jnp.concatenate([flux[:8], flux[8:]], axis=1)
        sent = flux.astype(BF16).astype(F32)
        empty = jnp.zeros_like(sent)
        for k in range(CAP):
            stack = [sent if j == k else empty for j in range(8)]
            fields.append(jnp.concatenate(stack, axis=0).astype(BF16))
    outgoing = mxu(names.astype(BF16), jnp.concatenate(fields, axis=1))
    for r in range(2 * CAP):
        boxes[plane(r), :] = outgoing[:, r * LANES : (r + 1) * LANES]
    for r in range(2 * CAP, ROWS):
        boxes[plane(r), :] = jnp.zeros((devices, LANES), F32)
    out_ref[...] = boxes[...].astype(BF16)


def combine(inbox, ocean):
    return pl.pallas_call(
        combine_kernel,
        in_specs=[VMEM, VMEM],
        out_specs=[VMEM, VMEM],
        out_shape=[
            jax.ShapeDtypeStruct(inbox.shape, BF16),
            jax.ShapeDtypeStruct((2, 8, 256), F32),
        ],
        scratch_shapes=[pltpu.VMEM(inbox.shape, F32)],
        compiler_params=params(24),
        name="ocean_flux",
    )(inbox, ocean)


def backward_kernel(
    place_ref, inbox_ref, w_ref, zero_ref, one_ref, _, out_ref,
    tiles_ref, picked, terms, held, sems, parts,
):
    tiles = place_ref.shape[1]
    arrivals = fetch_tiles(w_ref, tiles_ref, parts)
    per_row = WIDE // LANES
    place = column(place_ref[0:1].astype(F32)).astype(jnp.int32)
    inbox = inbox_ref[...]
    slot = iota((tiles, inbox.shape[0]), 1)
    for v in range(2):
        picked[v] = mxu(onehot(slot == place + v * CAP), inbox)
    scatter = onehot(iota((256, tiles), 0) == place_ref[1:2])

    for t in range(0, tiles, GROUP):
        weights = held_tiles(t, None, tiles_ref, arrivals)
        rows = slice(t, t + GROUP)
        pair = jnp.concatenate([picked[0, rows], picked[1, rows]], axis=0)
        wide = mxu(pair.astype(BF16), weights, ((1,), (1,)))
        both = 0.0
        for i in range(GROUP):
            both = both + masked(wide[:, i * LANES : (i + 1) * LANES], i)
        terms[0, rows] = both[:GROUP]
        terms[1, rows] = both[GROUP:]

    halves = [part for v in range(2) for part in split(terms[v])]
    summed = mxu(scatter, jnp.concatenate(halves, axis=1))
    copies = []
    for v, level_ref in enumerate((zero_ref, one_ref)):
        at = 2 * v * LANES
        returned = summed[:, at : at + LANES] + summed[:, at + LANES : at + 2 * LANES]
        for b in range(per_row):
            lanes = slice(b * LANES, (b + 1) * LANES)
            held[v, :, lanes] = level_ref[:, lanes] - couple * returned[b * 16 : (b + 1) * 16]
        copy = pltpu.make_async_copy(held.at[v], out_ref.at[v, pl.ds(0, 16)], sems.at[v])
        copy.start()
        copies.append(copy)
    for copy in copies:
        copy.wait()


def backward(place, inbox, weights, zero, one, atm, parts=4):
    tiles = weights.shape[0]
    return pl.pallas_call(
        backward_kernel,
        in_specs=[VMEM, VMEM, HBM, VMEM, VMEM, HBM],
        out_specs=HBM,
        out_shape=pltpu.HBM(atm.shape, F32),
        scratch_shapes=[
            pltpu.VMEM(weights.shape, BF16),
            pltpu.VMEM((2, tiles, LANES), F32),
            pltpu.VMEM((2, tiles, LANES), F32),
            pltpu.VMEM((2, 16, WIDE), F32),
            pltpu.SemaphoreType.DMA((2,)),
            pltpu.SemaphoreType.DMA((parts,)),
        ],
        input_output_aliases={5: 0},
        compiler_params=params(32),
        cost_estimate=cost(32 * tiles * LANES * LANES, 1),
        name="tiles_backward",
    )(place, inbox, weights, zero, one, atm)


def swap(rows):
    devices = lax.axis_size(RING)
    boxes = rows.reshape(devices, ROWS, LANES)
    return lax.all_to_all(boxes, RING, split_axis=0, concat_axis=0, tiled=True).reshape(rows.shape)


def per_device(
    atm_state,
    ocean_state,
    atm_levels,
    ocean_levels,
    tile_weight,
    tile_owner,
    tile_block,
    tile_source,
    tile_count,
):
    devices = lax.axis_size(RING)
    tiles = tile_weight.shape[0]
    atm = atm_state.reshape(2, 256, WIDE)
    ocean = ocean_state.reshape(2, 128, 256)
    grp, dom = lax.axis_index("grp"), lax.axis_index("dom")
    last = lax.axis_size("dom") - 1
    edge = jnp.stack([grp, (dom == 0).astype(jnp.int32), (dom == last).astype(jnp.int32)])

    atm = pltpu.with_memory_space_constraint(atm, pltpu.HBM)
    sea_state = pltpu.with_memory_space_constraint(ocean, pltpu.HBM)
    tile_weight = pltpu.with_memory_space_constraint(tile_weight, pltpu.HBM)
    lists = [x.reshape(1, tiles) for x in (tile_owner, tile_block, tile_source)]
    to_next, to_prev, level, ahead = pack(atm, sea_state, tile_weight)
    forth = [(i, (i + 1) % devices) for i in range(devices)]
    back = [(target, source) for source, target in forth]
    low = lax.ppermute(to_next, RING, forth)
    high = lax.ppermute(to_prev, RING, back)
    outbox, place = forward(
        tile_count.reshape(1, 1), *lists, level, ahead, tile_weight, devices
    )
    inbox = swap(outbox)
    columns = edge_rows(edge, ocean, low, high)
    side = lax.ppermute(columns, "grp", [(0, 1), (1, 0)])
    half, zero, halo, sea, own = early(edge, atm_levels, ocean_levels, atm, low, high)
    own = pltpu.with_memory_space_constraint(own, pltpu.HBM)
    inbox, half, side = lax.optimization_barrier((inbox, half, side))
    outgoing, flux = combine(inbox, ocean)
    returned = swap(outgoing)
    whole, one, ocean_final = late(
        edge, atm, ocean, low, high, side, flux, halo, sea, own, half
    )
    returned, whole, ocean_final = lax.optimization_barrier((returned, whole, ocean_final))
    atm_final = backward(place, returned, tile_weight, zero, one, whole)
    return atm_final.reshape(atm_state.shape), ocean_final.reshape(ocean_state.shape)


def solution(mesh):
    in_specs = (
        P(None, None, RING, None),
        P(None, None, "dom", "grp"),
        P(),
        P(),
        P(RING, None, None),
        P(RING, None),
        P(RING),
        P(RING),
        P(RING),
    )
    out_specs = (P(None, None, RING, None), P(None, None, "dom", "grp"))
    return jax.shard_map(
        per_device, mesh=mesh, in_specs=in_specs, out_specs=out_specs, check_vma=False
    )
```

```python
import functools
import math

import jax
import jax.numpy as jnp
from jax import lax
from jax.experimental import pallas as pl
from jax.experimental.pallas import tpu as pltpu
from jax.sharding import PartitionSpec as P

STEPS = 4
HALO = STEPS
CAP = 3
ROWS = 8
LANES = 128
GROUP = 8
PAD = 8
AHEAD = 64
WIDE = 2048
RING = ("grp", "dom")
F32 = jnp.float32
BF16 = jnp.bfloat16

diffuse = 0.2
vertical = 0.25
couple = 0.5
MIB = 1 << 20


VMEM = pl.BlockSpec(memory_space=pltpu.VMEM)
HBM = pl.BlockSpec(memory_space=pltpu.HBM)
SMEM = pl.BlockSpec(memory_space=pltpu.SMEM)


def params(mib):
    return pltpu.CompilerParams(vmem_limit_bytes=mib * MIB)


def cost(flops, mib):
    return pl.CostEstimate(flops=flops, bytes_accessed=mib * MIB, transcendentals=0)


def fetch(pairs, sems):
    copies = []
    for n, (source, target) in enumerate(pairs):
        copies.append(pltpu.make_async_copy(source, target, sems.at[n]))
        copies[-1].start()
    return copies


def iota(shape, dim):
    return lax.broadcasted_iota(jnp.int32, shape, dim)


def onehot(mask):
    return jnp.where(mask, 1.0, 0.0).astype(BF16)


def split(value):
    high = value.astype(BF16)
    return high, (value - high.astype(F32)).astype(BF16)


def mxu(left, right, dims=((1,), (0,))):
    return lax.dot_general(left, right, (dims, ((), ())), preferred_element_type=F32)


def exact(left, right):
    return lax.dot_general(
        left, right, (((1,), (0,)), ((), ())), precision=lax.Precision.HIGHEST,
        preferred_element_type=F32,
    )


def column(row):
    n = row.shape[1]
    eye = iota((n, n), 0) == iota((n, n), 1)
    return jnp.sum(jnp.where(eye, jnp.broadcast_to(row, (n, n)), 0.0), axis=1, keepdims=True)


def select_rows(state):
    rows = state.shape[0]
    deep = rows // 16
    out, col = iota((32 * HALO, rows), 0), iota((32 * HALO, rows), 1)
    first = ((out >> 2) & 15) * deep + (out & 3)
    return mxu(onehot(col == jnp.where(out < 16 * HALO, first + deep - HALO, first)), state)


def coefficients():
    table = []
    for s in range(STEPS):
        by_level = []
        for i in range(STEPS - s + 1):
            by_distance = [0.0] * (STEPS + 1)
            for k in range(s, STEPS - i + 1, 2):
                q = STEPS - k - i
                trinomial = [1]
                for _ in range(q):
                    padded = [0, 0] + trinomial + [0, 0]
                    trinomial = [sum(padded[j : j + 3]) for j in range(len(trinomial) + 2)]
                scale = math.comb(k, (k - s) // 2) * math.comb(STEPS, k)
                scale *= math.comb(STEPS - k, i) * diffuse ** (k + q)
                for d in range(q + 1):
                    by_distance[d] += scale * trinomial[q + d]
            by_level.append(by_distance)
        table.append(by_level)
    return table


def lookup(weights, distance):
    total = 0.0
    for d, weight in enumerate(weights):
        if weight:
            total = jnp.where(distance == d, weight, total)
    return total


def stencils(own, image):
    table = coefficients()
    x = iota((16, LANES), 1) & (own - 1)
    r = iota((16, LANES), 0)
    sources = [(r & (own - 1), own), ((r & 3) - HALO, HALO), ((r & 3) + own, HALO)]
    result = [[[] for _ in by_level] for by_level in table]
    for xs, depth in sources:
        distance = jnp.abs(xs - x)
        if image is not None:
            first, last = image
            below = jnp.where(first == 1, jnp.abs(xs + x + 2), STEPS + 1)
            above = jnp.where(last == 1, jnp.abs(2 * own - xs - x), STEPS + 1)
            inside = ((first == 0) | (xs >= 0)) & ((last == 0) | (xs < own))
        for s, by_level in enumerate(table):
            for i, weights in enumerate(by_level):
                part = lookup(weights, distance)
                if image is not None:
                    part = part - lookup(weights, below) - lookup(weights, above)
                    part = jnp.where(inside, part, 0.0)
                result[s][i] += [part] * depth
    return [[jnp.concatenate(parts, axis=0) for parts in by_level] for by_level in result]


def small_product(left, right):
    total = 0.0
    for k in range(16):
        total = total + left[:, k : k + 1] * right[k : k + 1, :]
    return total


def operators(levels, own, image):
    rows, cols = 16 * own + 32 * HALO, 16 * own
    shift = own.bit_length() - 1
    one = vertical * levels.T[:16]
    two = small_product(one, one)
    stack = [half for p in (one, two, small_product(two, one), small_product(two, two))
             for half in split(p)]
    stack = jnp.concatenate([half.astype(F32) for half in stack], axis=0).astype(BF16)
    spread = onehot(iota((LANES, cols), 0) == (iota((LANES, cols), 1) >> shift))
    wide = mxu(stack, spread).astype(BF16)
    r, c = iota((rows, LANES), 0), iota((rows, LANES), 1)
    level = jnp.where(r < cols, r >> shift, (r >> 2) & 15)
    mixed = [mxu(onehot(((c & 15) == level) & ((c >> 5) == i)), wide) for i in range(STEPS)]
    r, c = iota((rows, cols), 0), iota((rows, cols), 1)
    same = jnp.where(r < cols, r >> shift, (r >> 2) & 15) == (c >> shift)
    result = []
    for by_level in stencils(own, image):
        total = 0.0
        for i, part in enumerate(by_level):
            part = jnp.concatenate([part] * (cols // LANES), axis=1)
            total = total + (jnp.where(same, part, 0.0) if i == 0 else part * mixed[i - 1])
        result.append(total)
    return result


def write_atmos(levels, own_ref, halo_ref):
    for s, part in enumerate(operators(levels, 16, None)):
        high, low = split(part[:256])
        lanes = slice((s & 1) * 256, (s & 1) * 256 + 256)
        if s < 2:
            own_ref[0:256, lanes] = low
            own_ref[256:512, lanes] = high
        else:
            own_ref[512:768, lanes] = high
        halo_ref[:, s * 256 : (s + 1) * 256] = part[256:].astype(BF16)


def write_ocean(edge_ref, levels, ocean_ref):
    image = (edge_ref[1], edge_ref[2])
    for s, part in enumerate(operators(levels, 8, image)):
        lanes = slice(s * LANES, (s + 1) * LANES)
        high, low = split(part[:128])
        ocean_ref[0:128, lanes] = low
        ocean_ref[128:256, lanes] = high
        ocean_ref[256:384, lanes] = part[128:].astype(BF16)


OWN, FAR, SEA = (768, 512), (128, 1024), (384, 512)


def mirror_low(rows):
    r = iota(rows.shape, 0)
    total = jnp.zeros_like(rows)
    for j in range(3):
        total = jnp.where(r == 6 - j, -rows[j : j + 1], total)
    return total


def mirror_high(rows):
    r = iota(rows.shape, 0)
    total = jnp.zeros_like(rows)
    for j in range(3):
        total = jnp.where(r == 1 + j, -rows[7 - j : 8 - j], total)
    return total


def halo_rows(halo, v):
    half = 16 * HALO
    empty = jnp.zeros((half, halo.shape[1]), halo.dtype)
    blocks = []
    for side in range(2):
        part = halo[side * half : (side + 1) * half]
        blocks += [part, empty] if v == 0 else [empty, part]
    return jnp.concatenate(blocks, axis=0)


def atmos_steps(v, arrivals, x_ref, low_ref, high_ref, own_ref, halo_ref, out_ref, surface_ref,
                left, main, minor, w, held, sems):
    chunks = len(arrivals)
    size = WIDE // chunks
    main[0:512] = own_ref[0:512]
    main[512:768] = own_ref[256:512]
    main[768:1024] = halo_rows(halo_ref[:, 0:512], v)
    minor[0:256] = own_ref[512:768]
    minor[256:512] = halo_rows(halo_ref[:, 512:1024], v)
    copies = []
    for n in range(chunks + 1):
        if n < chunks:
            arrivals[n].wait()
            start = n * size
            for c in range(size // LANES):
                rows = slice(c * LANES, (c + 1) * LANES)
                at = start + c * LANES
                for h in range(2):
                    state = x_ref[h * LANES : (h + 1) * LANES, at : at + LANES].T
                    high, low = split(state)
                    lanes = slice(h * LANES, (h + 1) * LANES)
                    w[STEPS, PAD + at : PAD + at + LANES, lanes] = state * diffuse**STEPS
                    left[rows, h * LANES : (h + 1) * LANES] = high
                    left[rows, 256 + h * LANES : 256 + (h + 1) * LANES] = low
                    left[rows, 512 + h * LANES : 512 + (h + 1) * LANES] = high
            left[:, 768:896] = low_ref[start : start + size]
            left[:, 896:1024] = high_ref[start : start + size]
            rows = slice(PAD + start, PAD + start + size)
            for s in range(2):
                lanes = slice(s * 256, (s + 1) * 256)
                w[s, rows] = mxu(left[...], main[:, lanes])
                w[2 + s, rows] = mxu(left[:, 512:1024], minor[:, lanes])
        if n == 0:
            for s in range(1, STEPS + 1):
                w[s, 0:PAD] = mirror_low(w[s, PAD : 2 * PAD])
        if n == chunks - 1:
            for s in range(1, STEPS + 1):
                w[s, WIDE + PAD : WIDE + 2 * PAD] = mirror_high(w[s, WIDE : WIDE + PAD])
        if n > 0:
            start = (n - 1) * size
            for c in range(size // LANES):
                at = PAD + start + c * LANES
                for h in range(2):
                    lanes = slice(h * LANES, (h + 1) * LANES)
                    total = w[0, at : at + LANES, lanes]
                    for s in range(1, STEPS + 1):
                        total += w[s, at - s : at - s + LANES, lanes]
                        total += w[s, at + s : at + s + LANES, lanes]
                    held[lanes, at - PAD : at - PAD + LANES] = total.T
            cells = pl.ds(start, size)
            surface_ref[:, start : start + size] = held[0:16, start : start + size]
            copy = pltpu.make_async_copy(
                held.at[:, cells], out_ref.at[v, :, cells], sems.at[n - 1]
            )
            copy.start()
            copies.append(copy)
    return copies


def atmos_scratch(chunks):
    size = WIDE // chunks
    return [
        pltpu.VMEM((256, WIDE), F32),
        pltpu.SemaphoreType.DMA((chunks,)),
        pltpu.VMEM((size, 1024), BF16),
        pltpu.VMEM((1024, 512), BF16),
        pltpu.VMEM((512, 512), BF16),
        pltpu.VMEM((STEPS + 1, WIDE + 2 * PAD, 256), F32),
        pltpu.VMEM((256, WIDE), F32),
        pltpu.SemaphoreType.DMA((chunks,)),
    ]


def fetch_atmos(v, atm_ref, x_ref, sems):
    size = WIDE // sems.shape[0]
    cells = [pl.ds(n * size, size) for n in range(sems.shape[0])]
    copies = [
        pltpu.make_async_copy(atm_ref.at[v, :, c], x_ref.at[:, c], sems.at[n])
        for n, c in enumerate(cells)
    ]
    copies[0].start()
    return copies


def edge_kernel(edge_ref, ocean_ref, low_ref, high_ref, out_ref):
    first = edge_ref[0] == 0
    for v in range(2):
        before, after = ocean_ref[v, :, 0:LANES].T[:PAD], ocean_ref[v, :, LANES:].T[LANES - PAD :]
        out_ref[v * PAD : (v + 1) * PAD] = jnp.where(first, after, before)
    for n, ref in enumerate((low_ref, high_ref)):
        before, after = ref[WIDE : WIDE + 16], ref[WIDE + 240 : WIDE + 256]
        edge = jnp.where(first, after.astype(F32)[16 - PAD :], before.astype(F32)[:PAD])
        out_ref[(2 + n) * PAD : (3 + n) * PAD] = edge


def edge_rows(edge, ocean, low, high):
    return pl.pallas_call(
        edge_kernel,
        in_specs=[SMEM, VMEM, VMEM, VMEM],
        out_specs=VMEM,
        out_shape=jax.ShapeDtypeStruct((4 * PAD, LANES), F32),
        compiler_params=params(16),
        name="ocean_edge",
    )(edge, ocean, low, high)


def early_kernel(
    edge_ref, atm_levels_ref, ocean_levels_ref, atm_ref, low_ref, high_ref,
    out_ref, surface_ref, halo, sea, own_out, levels, own, few, *rest,
):
    x_ref, x_sems = rest[:2]
    arrivals = fetch_atmos(0, atm_ref, x_ref, x_sems)
    levels[...] = jnp.zeros_like(levels)
    levels[0, 0:16, 0:16] = atm_levels_ref[...]
    levels[1, 0:16, 0:16] = ocean_levels_ref[...]
    write_atmos(levels[0], own, halo)
    for copy in arrivals[1:]:
        copy.start()
    keep = fetch([(own, own_out)], few)
    sent = atmos_steps(
        0, arrivals, x_ref, low_ref, high_ref, own, halo, out_ref, surface_ref, *rest[2:]
    )
    write_ocean(edge_ref, levels[1], sea)
    for copy in keep + sent:
        copy.wait()


def early(edge, atm_levels, ocean_levels, atm, low, high, chunks=4):
    return pl.pallas_call(
        early_kernel,
        in_specs=[SMEM, VMEM, VMEM, HBM, VMEM, VMEM],
        out_specs=[HBM, VMEM, VMEM, VMEM, HBM],
        out_shape=[
            pltpu.HBM(atm.shape, F32),
            jax.ShapeDtypeStruct((16, WIDE), F32),
            jax.ShapeDtypeStruct(FAR, BF16),
            jax.ShapeDtypeStruct(SEA, BF16),
            pltpu.HBM(OWN, BF16),
        ],
        scratch_shapes=[
            pltpu.VMEM((2, LANES, LANES), F32),
            pltpu.VMEM(OWN, BF16),
            pltpu.SemaphoreType.DMA((1,)),
        ]
        + atmos_scratch(chunks),
        compiler_params=params(40),
        cost_estimate=cost(3 * 512 * 1024 * WIDE, 6),
        name="atmosphere_0",
    )(edge, atm_levels, ocean_levels, atm, low, high)


def ocean_steps(v, first, ocean_ref, low_ref, high_ref, side_ref, g_ref, flux_ref, out_ref, w):
    wide = ocean_ref.shape[2]

    def extend(rows, side):
        empty = jnp.zeros_like(side)
        before, after = jnp.where(first, empty, side), jnp.where(first, side, empty)
        return jnp.concatenate([before, rows, after], axis=0)

    halos = []
    for n, ref in enumerate((low_ref, high_ref)):
        side = side_ref[(2 + n) * PAD : (3 + n) * PAD]
        halos.append(extend(ref[WIDE : WIDE + wide].astype(F32), side).astype(BF16))
    own = jnp.concatenate([ocean_ref[v, :, :LANES].T, ocean_ref[v, :, LANES:].T], axis=0)
    state = extend(own, side_ref[v * PAD : (v + 1) * PAD])
    high, low = split(state)
    left = jnp.concatenate([high, low, high] + halos, axis=1)
    g = g_ref[...]
    right = jnp.concatenate([g[:256], g[128:256], halo_rows(g[256:], v)], axis=0)
    for s in range(0, STEPS, 2):
        both = mxu(left, right[:, s * LANES : (s + 2) * LANES])
        w[s], w[s + 1] = both[:, :LANES], both[:, LANES:]
    w[STEPS] = state * diffuse**STEPS
    end = wide + PAD
    for s in range(1, STEPS + 1):
        w[s, 0:PAD] = jnp.where(first, mirror_low(w[s, PAD : 2 * PAD]), w[s, 0:PAD])
        w[s, end : end + PAD] = jnp.where(
            first, w[s, end : end + PAD], mirror_high(w[s, end - PAD : end])
        )
    for c in range(wide // LANES):
        at = PAD + c * LANES
        total = w[0, at : at + LANES]
        for s in range(1, STEPS + 1):
            total += w[s, at - s : at - s + LANES]
            total += w[s, at + s : at + s + LANES]
        final = total.T
        lanes = slice(c * LANES, (c + 1) * LANES)
        out_ref[v, :, lanes] = final
        out_ref[v, 0:8, lanes] = final[0:8] + couple * flux_ref[v, :, lanes]


def late_kernel(
    edge_ref, atm_ref, ocean_ref, low_ref, high_ref, side_ref, flux_ref, halo_ref, sea_ref,
    own_ref, _, out_ref, surface_ref, ocean_out, own, sea_w, few, *rest,
):
    x_ref, x_sems = rest[:2]
    (arrival,) = fetch([(own_ref, own)], few)
    x_arrivals = fetch_atmos(1, atm_ref, x_ref, x_sems)
    ocean = (
        edge_ref[0] == 0, ocean_ref, low_ref, high_ref, side_ref, sea_ref, flux_ref, ocean_out,
        sea_w,
    )
    ocean_steps(0, *ocean)
    for copy in x_arrivals[1:]:
        copy.start()
    arrival.wait()
    sent = atmos_steps(
        1, x_arrivals, x_ref, low_ref, high_ref, own, halo_ref, out_ref, surface_ref, *rest[2:]
    )
    ocean_steps(1, *ocean)
    for copy in sent:
        copy.wait()


def late(edge, atm, ocean, low, high, side, flux, halo, sea, own, half, chunks=4):
    return pl.pallas_call(
        late_kernel,
        in_specs=[SMEM, HBM] + [VMEM] * 7 + [HBM] * 2,
        out_specs=[HBM, VMEM, VMEM],
        out_shape=[
            pltpu.HBM(atm.shape, F32),
            jax.ShapeDtypeStruct((16, WIDE), F32),
            jax.ShapeDtypeStruct(ocean.shape, F32),
        ],
        scratch_shapes=[
            pltpu.VMEM(OWN, BF16),
            pltpu.VMEM((STEPS + 1, ocean.shape[2] + 2 * PAD, LANES), F32),
            pltpu.SemaphoreType.DMA((1,)),
        ]
        + atmos_scratch(chunks),
        input_output_aliases={10: 0},
        compiler_params=params(40),
        cost_estimate=cost(3 * 512 * 1024 * WIDE, 6),
        name="atmosphere_1",
    )(edge, atm, ocean, low, high, side, flux, halo, sea, own, half)


def masked(pair, i):
    return jnp.where(iota(pair.shape, 0) % GROUP == i, pair, 0.0)


def send_rows(states, start, next_ref, prev_ref):
    picked = [select_rows(state) for state in states]
    half = 16 * HALO
    for rows, out_ref in ((slice(0, half), next_ref), (slice(half, None), prev_ref)):
        both = jnp.concatenate([part[rows] for part in picked], axis=0)
        for c in range(both.shape[1] // LANES):
            chunk = both[:, c * LANES : (c + 1) * LANES].T.astype(BF16)
            out_ref[start + c * LANES : start + (c + 1) * LANES] = chunk


def pack_kernel(
    atm_ref, ocean_ref, next_ref, prev_ref, level_ref, x_ref, sea_state, few, sems
):
    chunks = sems.shape[0]
    width = WIDE // chunks
    cells = [pl.ds(n * width, width) for n in range(chunks)]
    (arrival,) = fetch([(ocean_ref, sea_state)], few)
    copies = fetch([(atm_ref.at[:, :, c], x_ref.at[:, :, c]) for c in cells], sems)
    arrival.wait()
    send_rows([sea_state[v].astype(BF16) for v in range(2)], WIDE, next_ref, prev_ref)
    for n, copy in enumerate(copies):
        copy.wait()
        lanes = slice(n * width, (n + 1) * width)
        states = [x_ref[v, :, lanes].astype(BF16) for v in range(2)]
        send_rows(states, n * width, next_ref, prev_ref)
        level_ref[:, :, lanes] = x_ref[:, 0:16, lanes]


def pack(atm, ocean, chunks=2):
    rows = jax.ShapeDtypeStruct((WIDE + ocean.shape[2], LANES), BF16)
    return pl.pallas_call(
        pack_kernel,
        in_specs=[HBM, HBM],
        out_specs=[VMEM] * 3,
        out_shape=[
            rows,
            rows,
            jax.ShapeDtypeStruct((2, 16, WIDE), F32),
        ],
        scratch_shapes=[
            pltpu.VMEM(atm.shape, F32),
            pltpu.VMEM(ocean.shape, F32),
            pltpu.SemaphoreType.DMA((1,)),
            pltpu.SemaphoreType.DMA((chunks,)),
        ],
        compiler_params=params(24),
        cost_estimate=cost(1 << 33, 16),
        name="pack_halo",
    )(atm, ocean)


def fetch_tiles(w_ref, tiles_ref, sems):
    count = tiles_ref.shape[0]
    first, size = w_ref.shape[0] - count, count // sems.shape[0]
    starts = [n * size for n in range(sems.shape[0])]
    return fetch(
        [(w_ref.at[pl.ds(first + t, size)], tiles_ref.at[pl.ds(t, size)]) for t in starts], sems
    )


def held_tiles(t, ahead_ref, tiles_ref, copies):
    ahead = 0 if ahead_ref is None else ahead_ref.shape[0]
    if t < ahead:
        held = ahead_ref[t : t + GROUP]
    else:
        size = tiles_ref.shape[0] // len(copies)
        if (t - ahead) % size == 0:
            copies[(t - ahead) // size].wait()
        held = tiles_ref[t - ahead : t - ahead + GROUP]
    return held.reshape(GROUP * LANES, LANES)


def forward_kernel(
    count_ref, owner_ref, block_ref, source_ref, level_ref, w_ref, out_ref, place_ref,
    picked, contrib, left,
):
    tiles = owner_ref.shape[1]
    per_row = WIDE // LANES

    source = source_ref[...]
    cell = (source & (per_row - 1)) * 16 + (source >> (per_row.bit_length() - 1))
    gather = onehot(iota((tiles, 256), 1).astype(F32) == column(cell.astype(F32)))
    for v in range(2):
        rounded = level_ref[v].astype(BF16)
        blocks = [rounded[:, b * LANES : (b + 1) * LANES] for b in range(per_row)]
        picked[v] = mxu(gather, jnp.concatenate(blocks, axis=0))
    owner = owner_ref[...].astype(F32)
    earlier = (column(owner) == owner) & (iota((tiles, tiles), 0) < iota((tiles, tiles), 1))
    rank = jnp.sum(jnp.where(earlier, 1.0, 0.0), axis=0, keepdims=True)
    live = iota((1, tiles), 1) < count_ref[...]
    place = jnp.where(live, owner_ref[...] * ROWS + rank.astype(jnp.int32), -64)
    index = jnp.where(live, owner_ref[...] * ROWS + 2 * CAP, -64)
    place_ref[0:1] = place
    place_ref[1:2] = jnp.where(live, cell, -64)
    place_ref[2:8] = jnp.zeros((6, tiles), jnp.int32)
    block = block_ref[...]
    lane = column(rank * 16.0 + ((block & 1) * 8 + (block >> 1)).astype(F32))
    names = onehot(iota((tiles, LANES), 1).astype(F32) == lane)
    part = out_ref.shape[0] * GROUP // tiles

    for t in range(0, tiles, GROUP):
        held = w_ref[t : t + GROUP].reshape(GROUP * LANES, LANES)
        row = iota((part, tiles), 0) + t // GROUP * part
        here = slice(t // GROUP * part, (t // GROUP + 1) * part)
        for m, at in enumerate((place, place + CAP, index)):
            left[here, m * tiles : (m + 1) * tiles] = onehot(row == at)
        rows = slice(t, t + GROUP)
        pair = jnp.concatenate([picked[0, rows], picked[1, rows]], axis=0)
        spread = jnp.concatenate([masked(pair, i).astype(BF16) for i in range(GROUP)], axis=1)
        both = mxu(spread, held)
        contrib[0, rows] = both[:GROUP]
        contrib[1, rows] = both[GROUP:]

    first = jnp.concatenate(split(contrib[0]), axis=1)
    second = jnp.concatenate(split(contrib[1]), axis=1)
    third = jnp.concatenate([names, jnp.zeros_like(names)], axis=1)
    out = mxu(left[...], jnp.concatenate([first, second, third], axis=0))
    out_ref[...] = out[:, :LANES] + out[:, LANES:]


def forward(count, owner, block, source, level, weights, devices):
    tiles = weights.shape[0]
    return pl.pallas_call(
        forward_kernel,
        in_specs=[VMEM] * 6,
        out_specs=[VMEM] * 2,
        out_shape=[
            jax.ShapeDtypeStruct((devices * ROWS, LANES), F32),
            jax.ShapeDtypeStruct((8, tiles), jnp.int32),
        ],
        scratch_shapes=[
            pltpu.VMEM((2, tiles, LANES), F32),
            pltpu.VMEM((2, tiles, LANES), F32),
            pltpu.VMEM((devices * ROWS, 3 * tiles), BF16),
        ],
        compiler_params=params(32),
        cost_estimate=cost(32 * tiles * LANES * LANES, 9),
        name="tiles_forward",
    )(count, owner, block, source, level, weights)


def combine_kernel(inbox_ref, ocean_ref, out_ref, flux_ref, boxes):
    devices = inbox_ref.shape[0] // ROWS

    def plane(r):
        return pl.ds(r, devices, stride=ROWS)

    names = inbox_ref[plane(6), :]
    parts = []
    for r in range(2 * CAP):
        value = inbox_ref[plane(r), :]
        high, low = split(value)
        rest = (value - high.astype(F32) - low.astype(F32)).astype(BF16)
        parts += [high, low, rest]
    summed = mxu(names.T.astype(BF16), jnp.concatenate(parts, axis=1))
    fields = []
    for v in range(2):
        received = 0.0
        for k in range(CAP):
            rows = summed[k * 16 : (k + 1) * 16]
            for term in range(3):
                at = ((v * CAP + k) * 3 + term) * LANES
                received = received + rows[:, at : at + LANES]
        surface = ocean_ref[v, 0:8]
        flux = received - jnp.concatenate([surface[:, :LANES], surface[:, LANES:]], axis=0)
        flux_ref[v] = jnp.concatenate([flux[:8], flux[8:]], axis=1)
        sent = flux.astype(BF16).astype(F32)
        empty = jnp.zeros_like(sent)
        for k in range(CAP):
            stack = [sent if j == k else empty for j in range(8)]
            fields.append(jnp.concatenate(stack, axis=0).astype(BF16))
    outgoing = mxu(names.astype(BF16), jnp.concatenate(fields, axis=1))
    for r in range(2 * CAP):
        boxes[plane(r), :] = outgoing[:, r * LANES : (r + 1) * LANES]
    for r in range(2 * CAP, ROWS):
        boxes[plane(r), :] = jnp.zeros((devices, LANES), F32)
    out_ref[...] = boxes[...].astype(BF16)


def combine(inbox, ocean):
    return pl.pallas_call(
        combine_kernel,
        in_specs=[VMEM, VMEM],
        out_specs=[VMEM, VMEM],
        out_shape=[
            jax.ShapeDtypeStruct(inbox.shape, BF16),
            jax.ShapeDtypeStruct((2, 8, 256), F32),
        ],
        scratch_shapes=[pltpu.VMEM(inbox.shape, F32)],
        compiler_params=params(24),
        name="ocean_flux",
    )(inbox, ocean)


def backward_kernel(
    place_ref, inbox_ref, w_ref, zero_ref, one_ref, _, out_ref,
    tiles_ref, picked, terms, held, sems, parts,
):
    tiles = place_ref.shape[1]
    arrivals = fetch_tiles(w_ref, tiles_ref, parts)
    per_row = WIDE // LANES
    place = column(place_ref[0:1].astype(F32)).astype(jnp.int32)
    inbox = inbox_ref[...]
    slot = iota((tiles, inbox.shape[0]), 1)
    for v in range(2):
        picked[v] = mxu(onehot(slot == place + v * CAP), inbox)
    scatter = onehot(iota((256, tiles), 0) == place_ref[1:2])

    for t in range(0, tiles, GROUP):
        weights = held_tiles(t, None, tiles_ref, arrivals)
        rows = slice(t, t + GROUP)
        pair = jnp.concatenate([picked[0, rows], picked[1, rows]], axis=0)
        wide = mxu(pair.astype(BF16), weights, ((1,), (1,)))
        both = 0.0
        for i in range(GROUP):
            both = both + masked(wide[:, i * LANES : (i + 1) * LANES], i)
        terms[0, rows] = both[:GROUP]
        terms[1, rows] = both[GROUP:]

    halves = [part for v in range(2) for part in split(terms[v])]
    summed = mxu(scatter, jnp.concatenate(halves, axis=1))
    copies = []
    for v, level_ref in enumerate((zero_ref, one_ref)):
        at = 2 * v * LANES
        returned = summed[:, at : at + LANES] + summed[:, at + LANES : at + 2 * LANES]
        for b in range(per_row):
            lanes = slice(b * LANES, (b + 1) * LANES)
            held[v, :, lanes] = level_ref[:, lanes] - couple * returned[b * 16 : (b + 1) * 16]
        copy = pltpu.make_async_copy(held.at[v], out_ref.at[v, pl.ds(0, 16)], sems.at[v])
        copy.start()
        copies.append(copy)
    for copy in copies:
        copy.wait()


def backward(place, inbox, weights, zero, one, atm, parts=4):
    tiles = weights.shape[0]
    return pl.pallas_call(
        backward_kernel,
        in_specs=[VMEM, VMEM, HBM, VMEM, VMEM, HBM],
        out_specs=HBM,
        out_shape=pltpu.HBM(atm.shape, F32),
        scratch_shapes=[
            pltpu.VMEM(weights.shape, BF16),
            pltpu.VMEM((2, tiles, LANES), F32),
            pltpu.VMEM((2, tiles, LANES), F32),
            pltpu.VMEM((2, 16, WIDE), F32),
            pltpu.SemaphoreType.DMA((2,)),
            pltpu.SemaphoreType.DMA((parts,)),
        ],
        input_output_aliases={5: 0},
        compiler_params=params(32),
        cost_estimate=cost(32 * tiles * LANES * LANES, 1),
        name="tiles_backward",
    )(place, inbox, weights, zero, one, atm)


def swap(rows):
    devices = lax.axis_size(RING)
    boxes = rows.reshape(devices, ROWS, LANES)
    return lax.all_to_all(boxes, RING, split_axis=0, concat_axis=0, tiled=True).reshape(rows.shape)


def per_device(
    atm_state,
    ocean_state,
    atm_levels,
    ocean_levels,
    tile_weight,
    tile_owner,
    tile_block,
    tile_source,
    tile_count,
):
    devices = lax.axis_size(RING)
    tiles = tile_weight.shape[0]
    atm = atm_state.reshape(2, 256, WIDE)
    ocean = ocean_state.reshape(2, 128, 256)
    grp, dom = lax.axis_index("grp"), lax.axis_index("dom")
    last = lax.axis_size("dom") - 1
    edge = jnp.stack([grp, (dom == 0).astype(jnp.int32), (dom == last).astype(jnp.int32)])

    atm = pltpu.with_memory_space_constraint(atm, pltpu.HBM)
    sea_state = pltpu.with_memory_space_constraint(ocean, pltpu.HBM)
    again = pltpu.with_memory_space_constraint(tile_weight, pltpu.HBM)
    lists = [x.reshape(1, tiles) for x in (tile_owner, tile_block, tile_source)]
    to_next, to_prev, level = pack(atm, sea_state)
    forth = [(i, (i + 1) % devices) for i in range(devices)]
    back = [(target, source) for source, target in forth]
    low = lax.ppermute(to_next, RING, forth)
    high = lax.ppermute(to_prev, RING, back)
    outbox, place = forward(
        tile_count.reshape(1, 1), *lists, level, tile_weight, devices
    )
    inbox = swap(outbox)
    columns = edge_rows(edge, ocean, low, high)
    side = lax.ppermute(columns, "grp", [(0, 1), (1, 0)])
    half, zero, halo, sea, own = early(edge, atm_levels, ocean_levels, atm, low, high)
    own = pltpu.with_memory_space_constraint(own, pltpu.HBM)
    inbox, half, side = lax.optimization_barrier((inbox, half, side))
    outgoing, flux = combine(inbox, ocean)
    returned = swap(outgoing)
    whole, one, ocean_final = late(
        edge, atm, ocean, low, high, side, flux, halo, sea, own, half
    )
    returned, whole, ocean_final = lax.optimization_barrier((returned, whole, ocean_final))
    atm_final = backward(place, returned, again, zero, one, whole)
    return atm_final.reshape(atm_state.shape), ocean_final.reshape(ocean_state.shape)


def solution(mesh):
    in_specs = (
        P(None, None, RING, None),
        P(None, None, "dom", "grp"),
        P(),
        P(),
        P(RING, None, None),
        P(RING, None),
        P(RING),
        P(RING),
        P(RING),
    )
    out_specs = (P(None, None, RING, None), P(None, None, "dom", "grp"))
    return jax.shard_map(
        per_device, mesh=mesh, in_specs=in_specs, out_specs=out_specs, check_vma=False
    )
```

```python
import functools
import math

import jax
import jax.numpy as jnp
from jax import lax
from jax.experimental import pallas as pl
from jax.experimental.pallas import tpu as pltpu
from jax.sharding import PartitionSpec as P

STEPS = 4
HALO = STEPS
CAP = 3
ROWS = 8
LANES = 128
GROUP = 8
PAD = 8
AHEAD = 64
WIDE = 2048
RING = ("grp", "dom")
F32 = jnp.float32
BF16 = jnp.bfloat16

diffuse = 0.2
vertical = 0.25
couple = 0.5
MIB = 1 << 20


VMEM = pl.BlockSpec(memory_space=pltpu.VMEM)
HBM = pl.BlockSpec(memory_space=pltpu.HBM)
SMEM = pl.BlockSpec(memory_space=pltpu.SMEM)


def params(mib):
    return pltpu.CompilerParams(vmem_limit_bytes=mib * MIB)


def cost(flops, mib):
    return pl.CostEstimate(flops=flops, bytes_accessed=mib * MIB, transcendentals=0)


def fetch(pairs, sems):
    copies = []
    for n, (source, target) in enumerate(pairs):
        copies.append(pltpu.make_async_copy(source, target, sems.at[n]))
        copies[-1].start()
    return copies


def iota(shape, dim):
    return lax.broadcasted_iota(jnp.int32, shape, dim)


def onehot(mask):
    return jnp.where(mask, 1.0, 0.0).astype(BF16)


def split(value):
    high = value.astype(BF16)
    return high, (value - high.astype(F32)).astype(BF16)


def mxu(left, right, dims=((1,), (0,))):
    return lax.dot_general(left, right, (dims, ((), ())), preferred_element_type=F32)


def exact(left, right):
    return lax.dot_general(
        left, right, (((1,), (0,)), ((), ())), precision=lax.Precision.HIGHEST,
        preferred_element_type=F32,
    )


def column(row):
    n = row.shape[1]
    eye = iota((n, n), 0) == iota((n, n), 1)
    return jnp.sum(jnp.where(eye, jnp.broadcast_to(row, (n, n)), 0.0), axis=1, keepdims=True)


def select_rows(state):
    rows = state.shape[0]
    deep = rows // 16
    out, col = iota((32 * HALO, rows), 0), iota((32 * HALO, rows), 1)
    first = ((out >> 2) & 15) * deep + (out & 3)
    return mxu(onehot(col == jnp.where(out < 16 * HALO, first + deep - HALO, first)), state)


def coefficients():
    table = []
    for s in range(STEPS):
        by_level = []
        for i in range(STEPS - s + 1):
            by_distance = [0.0] * (STEPS + 1)
            for k in range(s, STEPS - i + 1, 2):
                q = STEPS - k - i
                trinomial = [1]
                for _ in range(q):
                    padded = [0, 0] + trinomial + [0, 0]
                    trinomial = [sum(padded[j : j + 3]) for j in range(len(trinomial) + 2)]
                scale = math.comb(k, (k - s) // 2) * math.comb(STEPS, k)
                scale *= math.comb(STEPS - k, i) * diffuse ** (k + q)
                for d in range(q + 1):
                    by_distance[d] += scale * trinomial[q + d]
            by_level.append(by_distance)
        table.append(by_level)
    return table


def lookup(weights, distance):
    total = 0.0
    for d, weight in enumerate(weights):
        if weight:
            total = jnp.where(distance == d, weight, total)
    return total


def stencils(own, image):
    table = coefficients()
    x = iota((16, LANES), 1) & (own - 1)
    r = iota((16, LANES), 0)
    sources = [(r & (own - 1), own), ((r & 3) - HALO, HALO), ((r & 3) + own, HALO)]
    result = [[[] for _ in by_level] for by_level in table]
    for xs, depth in sources:
        distance = jnp.abs(xs - x)
        if image is not None:
            first, last = image
            below = jnp.where(first == 1, jnp.abs(xs + x + 2), STEPS + 1)
            above = jnp.where(last == 1, jnp.abs(2 * own - xs - x), STEPS + 1)
            inside = ((first == 0) | (xs >= 0)) & ((last == 0) | (xs < own))
        for s, by_level in enumerate(table):
            for i, weights in enumerate(by_level):
                part = lookup(weights, distance)
                if image is not None:
                    part = part - lookup(weights, below) - lookup(weights, above)
                    part = jnp.where(inside, part, 0.0)
                result[s][i] += [part] * depth
    return [[jnp.concatenate(parts, axis=0) for parts in by_level] for by_level in result]


def small_product(left, right):
    total = 0.0
    for k in range(16):
        total = total + left[:, k : k + 1] * right[k : k + 1, :]
    return total


def operators(levels, own, image):
    rows, cols = 16 * own + 32 * HALO, 16 * own
    shift = own.bit_length() - 1
    one = vertical * levels.T[:16]
    two = small_product(one, one)
    stack = [half for p in (one, two, small_product(two, one), small_product(two, two))
             for half in split(p)]
    stack = jnp.concatenate([half.astype(F32) for half in stack], axis=0).astype(BF16)
    spread = onehot(iota((LANES, cols), 0) == (iota((LANES, cols), 1) >> shift))
    wide = mxu(stack, spread).astype(BF16)
    r, c = iota((rows, LANES), 0), iota((rows, LANES), 1)
    level = jnp.where(r < cols, r >> shift, (r >> 2) & 15)
    mixed = [mxu(onehot(((c & 15) == level) & ((c >> 5) == i)), wide) for i in range(STEPS)]
    r, c = iota((rows, cols), 0), iota((rows, cols), 1)
    same = jnp.where(r < cols, r >> shift, (r >> 2) & 15) == (c >> shift)
    result = []
    for by_level in stencils(own, image):
        total = 0.0
        for i, part in enumerate(by_level):
            part = jnp.concatenate([part] * (cols // LANES), axis=1)
            total = total + (jnp.where(same, part, 0.0) if i == 0 else part * mixed[i - 1])
        result.append(total)
    return result


def write_atmos(levels, own_ref, halo_ref):
    for s, part in enumerate(operators(levels, 16, None)):
        high, low = split(part[:256])
        lanes = slice((s & 1) * 256, (s & 1) * 256 + 256)
        if s < 2:
            own_ref[0:256, lanes] = low
            own_ref[256:512, lanes] = high
        else:
            own_ref[512:768, lanes] = high
        halo_ref[:, s * 256 : (s + 1) * 256] = part[256:].astype(BF16)


def write_ocean(edge_ref, levels, ocean_ref):
    image = (edge_ref[1], edge_ref[2])
    for s, part in enumerate(operators(levels, 8, image)):
        lanes = slice(s * LANES, (s + 1) * LANES)
        high, low = split(part[:128])
        ocean_ref[0:128, lanes] = low
        ocean_ref[128:256, lanes] = high
        ocean_ref[256:384, lanes] = part[128:].astype(BF16)


OWN, FAR, SEA = (768, 512), (128, 1024), (384, 512)


def mirror_low(rows):
    r = iota(rows.shape, 0)
    total = jnp.zeros_like(rows)
    for j in range(3):
        total = jnp.where(r == 6 - j, -rows[j : j + 1], total)
    return total


def mirror_high(rows):
    r = iota(rows.shape, 0)
    total = jnp.zeros_like(rows)
    for j in range(3):
        total = jnp.where(r == 1 + j, -rows[7 - j : 8 - j], total)
    return total


def halo_rows(halo, v):
    half = 16 * HALO
    empty = jnp.zeros((half, halo.shape[1]), halo.dtype)
    blocks = []
    for side in range(2):
        part = halo[side * half : (side + 1) * half]
        blocks += [part, empty] if v == 0 else [empty, part]
    return jnp.concatenate(blocks, axis=0)


def atmos_steps(v, arrivals, x_ref, low_ref, high_ref, own_ref, halo_ref, out_ref, surface_ref,
                left, main, minor, w, held, sems):
    chunks = len(arrivals)
    size = WIDE // chunks
    main[0:256] = own_ref[256:512]
    main[256:512] = own_ref[256:512]
    main[512:768] = halo_rows(halo_ref[:, 0:512], v)
    minor[0:256] = own_ref[512:768]
    minor[256:512] = halo_rows(halo_ref[:, 512:1024], v)
    copies = []
    for n in range(chunks + 1):
        if n < chunks:
            arrivals[n].wait()
            start = n * size
            for c in range(size // LANES):
                rows = slice(c * LANES, (c + 1) * LANES)
                at = start + c * LANES
                for h in range(2):
                    state = x_ref[h * LANES : (h + 1) * LANES, at : at + LANES].T
                    high, low = split(state)
                    lanes = slice(h * LANES, (h + 1) * LANES)
                    w[STEPS, PAD + at : PAD + at + LANES, lanes] = state * diffuse**STEPS
                    left[rows, h * LANES : (h + 1) * LANES] = low
                    left[rows, 256 + h * LANES : 256 + (h + 1) * LANES] = high
            left[:, 512:640] = low_ref[start : start + size]
            left[:, 640:768] = high_ref[start : start + size]
            rows = slice(PAD + start, PAD + start + size)
            for s in range(2):
                lanes = slice(s * 256, (s + 1) * 256)
                fine = mxu(left[:, 256:512], own_ref[0:256, lanes])
                w[s, rows] = mxu(left[...], main[:, lanes]) + fine
                w[2 + s, rows] = mxu(left[:, 256:768], minor[:, lanes])
        if n == 0:
            for s in range(1, STEPS + 1):
                w[s, 0:PAD] = mirror_low(w[s, PAD : 2 * PAD])
        if n == chunks - 1:
            for s in range(1, STEPS + 1):
                w[s, WIDE + PAD : WIDE + 2 * PAD] = mirror_high(w[s, WIDE : WIDE + PAD])
        if n > 0:
            start = (n - 1) * size
            for c in range(size // LANES):
                at = PAD + start + c * LANES
                for h in range(2):
                    lanes = slice(h * LANES, (h + 1) * LANES)
                    total = w[0, at : at + LANES, lanes]
                    for s in range(1, STEPS + 1):
                        total += w[s, at - s : at - s + LANES, lanes]
                        total += w[s, at + s : at + s + LANES, lanes]
                    held[lanes, at - PAD : at - PAD + LANES] = total.T
            cells = pl.ds(start, size)
            surface_ref[:, start : start + size] = held[0:16, start : start + size]
            copy = pltpu.make_async_copy(
                held.at[:, cells], out_ref.at[v, :, cells], sems.at[n - 1]
            )
            copy.start()
            copies.append(copy)
    return copies


def atmos_scratch(chunks):
    size = WIDE // chunks
    return [
        pltpu.VMEM((256, WIDE), F32),
        pltpu.SemaphoreType.DMA((chunks,)),
        pltpu.VMEM((size, 768), BF16),
        pltpu.VMEM((768, 512), BF16),
        pltpu.VMEM((512, 512), BF16),
        pltpu.VMEM((STEPS + 1, WIDE + 2 * PAD, 256), F32),
        pltpu.VMEM((256, WIDE), F32),
        pltpu.SemaphoreType.DMA((chunks,)),
    ]


def fetch_atmos(v, atm_ref, x_ref, sems):
    size = WIDE // sems.shape[0]
    cells = [pl.ds(n * size, size) for n in range(sems.shape[0])]
    copies = [
        pltpu.make_async_copy(atm_ref.at[v, :, c], x_ref.at[:, c], sems.at[n])
        for n, c in enumerate(cells)
    ]
    copies[0].start()
    return copies


def edge_kernel(edge_ref, ocean_ref, low_ref, high_ref, out_ref):
    first = edge_ref[0] == 0
    for v in range(2):
        before, after = ocean_ref[v, :, 0:LANES].T[:PAD], ocean_ref[v, :, LANES:].T[LANES - PAD :]
        out_ref[v * PAD : (v + 1) * PAD] = jnp.where(first, after, before)
    for n, ref in enumerate((low_ref, high_ref)):
        before, after = ref[WIDE : WIDE + 16], ref[WIDE + 240 : WIDE + 256]
        edge = jnp.where(first, after.astype(F32)[16 - PAD :], before.astype(F32)[:PAD])
        out_ref[(2 + n) * PAD : (3 + n) * PAD] = edge


def edge_rows(edge, ocean, low, high):
    return pl.pallas_call(
        edge_kernel,
        in_specs=[SMEM, VMEM, VMEM, VMEM],
        out_specs=VMEM,
        out_shape=jax.ShapeDtypeStruct((4 * PAD, LANES), F32),
        compiler_params=params(16),
        name="ocean_edge",
    )(edge, ocean, low, high)


def early_kernel(
    edge_ref, atm_levels_ref, ocean_levels_ref, atm_ref, low_ref, high_ref,
    out_ref, surface_ref, halo, sea, own_out, levels, own, few, *rest,
):
    x_ref, x_sems = rest[:2]
    arrivals = fetch_atmos(0, atm_ref, x_ref, x_sems)
    levels[...] = jnp.zeros_like(levels)
    levels[0, 0:16, 0:16] = atm_levels_ref[...]
    levels[1, 0:16, 0:16] = ocean_levels_ref[...]
    write_atmos(levels[0], own, halo)
    for copy in arrivals[1:]:
        copy.start()
    keep = fetch([(own, own_out)], few)
    sent = atmos_steps(
        0, arrivals, x_ref, low_ref, high_ref, own, halo, out_ref, surface_ref, *rest[2:]
    )
    write_ocean(edge_ref, levels[1], sea)
    for copy in keep + sent:
        copy.wait()


def early(edge, atm_levels, ocean_levels, atm, low, high, chunks=4):
    return pl.pallas_call(
        early_kernel,
        in_specs=[SMEM, VMEM, VMEM, HBM, VMEM, VMEM],
        out_specs=[HBM, VMEM, VMEM, VMEM, HBM],
        out_shape=[
            pltpu.HBM(atm.shape, F32),
            jax.ShapeDtypeStruct((16, WIDE), F32),
            jax.ShapeDtypeStruct(FAR, BF16),
            jax.ShapeDtypeStruct(SEA, BF16),
            pltpu.HBM(OWN, BF16),
        ],
        scratch_shapes=[
            pltpu.VMEM((2, LANES, LANES), F32),
            pltpu.VMEM(OWN, BF16),
            pltpu.SemaphoreType.DMA((1,)),
        ]
        + atmos_scratch(chunks),
        compiler_params=params(40),
        cost_estimate=cost(3 * 512 * 1024 * WIDE, 6),
        name="atmosphere_0",
    )(edge, atm_levels, ocean_levels, atm, low, high)


def ocean_steps(v, first, ocean_ref, low_ref, high_ref, side_ref, g_ref, flux_ref, out_ref, w):
    wide = ocean_ref.shape[2]

    def extend(rows, side):
        empty = jnp.zeros_like(side)
        before, after = jnp.where(first, empty, side), jnp.where(first, side, empty)
        return jnp.concatenate([before, rows, after], axis=0)

    halos = []
    for n, ref in enumerate((low_ref, high_ref)):
        side = side_ref[(2 + n) * PAD : (3 + n) * PAD]
        halos.append(extend(ref[WIDE : WIDE + wide].astype(F32), side).astype(BF16))
    own = jnp.concatenate([ocean_ref[v, :, :LANES].T, ocean_ref[v, :, LANES:].T], axis=0)
    state = extend(own, side_ref[v * PAD : (v + 1) * PAD])
    high, low = split(state)
    left = jnp.concatenate([high, low, high] + halos, axis=1)
    g = g_ref[...]
    right = jnp.concatenate([g[:256], g[128:256], halo_rows(g[256:], v)], axis=0)
    for s in range(0, STEPS, 2):
        both = mxu(left, right[:, s * LANES : (s + 2) * LANES])
        w[s], w[s + 1] = both[:, :LANES], both[:, LANES:]
    w[STEPS] = state * diffuse**STEPS
    end = wide + PAD
    for s in range(1, STEPS + 1):
        w[s, 0:PAD] = jnp.where(first, mirror_low(w[s, PAD : 2 * PAD]), w[s, 0:PAD])
        w[s, end : end + PAD] = jnp.where(
            first, w[s, end : end + PAD], mirror_high(w[s, end - PAD : end])
        )
    for c in range(wide // LANES):
        at = PAD + c * LANES
        total = w[0, at : at + LANES]
        for s in range(1, STEPS + 1):
            total += w[s, at - s : at - s + LANES]
            total += w[s, at + s : at + s + LANES]
        final = total.T
        lanes = slice(c * LANES, (c + 1) * LANES)
        out_ref[v, :, lanes] = final
        out_ref[v, 0:8, lanes] = final[0:8] + couple * flux_ref[v, :, lanes]


def late_kernel(
    edge_ref, atm_ref, ocean_ref, low_ref, high_ref, side_ref, flux_ref, halo_ref, sea_ref,
    own_ref, _, out_ref, surface_ref, ocean_out, own, sea_w, few, *rest,
):
    x_ref, x_sems = rest[:2]
    (arrival,) = fetch([(own_ref, own)], few)
    x_arrivals = fetch_atmos(1, atm_ref, x_ref, x_sems)
    ocean = (
        edge_ref[0] == 0, ocean_ref, low_ref, high_ref, side_ref, sea_ref, flux_ref, ocean_out,
        sea_w,
    )
    ocean_steps(0, *ocean)
    for copy in x_arrivals[1:]:
        copy.start()
    arrival.wait()
    sent = atmos_steps(
        1, x_arrivals, x_ref, low_ref, high_ref, own, halo_ref, out_ref, surface_ref, *rest[2:]
    )
    ocean_steps(1, *ocean)
    for copy in sent:
        copy.wait()


def late(edge, atm, ocean, low, high, side, flux, halo, sea, own, half, chunks=4):
    return pl.pallas_call(
        late_kernel,
        in_specs=[SMEM, HBM] + [VMEM] * 7 + [HBM] * 2,
        out_specs=[HBM, VMEM, VMEM],
        out_shape=[
            pltpu.HBM(atm.shape, F32),
            jax.ShapeDtypeStruct((16, WIDE), F32),
            jax.ShapeDtypeStruct(ocean.shape, F32),
        ],
        scratch_shapes=[
            pltpu.VMEM(OWN, BF16),
            pltpu.VMEM((STEPS + 1, ocean.shape[2] + 2 * PAD, LANES), F32),
            pltpu.SemaphoreType.DMA((1,)),
        ]
        + atmos_scratch(chunks),
        input_output_aliases={10: 0},
        compiler_params=params(40),
        cost_estimate=cost(3 * 512 * 1024 * WIDE, 6),
        name="atmosphere_1",
    )(edge, atm, ocean, low, high, side, flux, halo, sea, own, half)


def masked(pair, i):
    return jnp.where(iota(pair.shape, 0) % GROUP == i, pair, 0.0)


def send_rows(states, start, next_ref, prev_ref):
    picked = [select_rows(state) for state in states]
    half = 16 * HALO
    for rows, out_ref in ((slice(0, half), next_ref), (slice(half, None), prev_ref)):
        both = jnp.concatenate([part[rows] for part in picked], axis=0)
        for c in range(both.shape[1] // LANES):
            chunk = both[:, c * LANES : (c + 1) * LANES].T.astype(BF16)
            out_ref[start + c * LANES : start + (c + 1) * LANES] = chunk


def pack_kernel(
    atm_ref, ocean_ref, next_ref, prev_ref, level_ref, x_ref, sea_state, few, sems
):
    chunks = sems.shape[0]
    width = WIDE // chunks
    cells = [pl.ds(n * width, width) for n in range(chunks)]
    (arrival,) = fetch([(ocean_ref, sea_state)], few)
    copies = fetch([(atm_ref.at[:, :, c], x_ref.at[:, :, c]) for c in cells], sems)
    arrival.wait()
    send_rows([sea_state[v].astype(BF16) for v in range(2)], WIDE, next_ref, prev_ref)
    for n, copy in enumerate(copies):
        copy.wait()
        lanes = slice(n * width, (n + 1) * width)
        states = [x_ref[v, :, lanes].astype(BF16) for v in range(2)]
        send_rows(states, n * width, next_ref, prev_ref)
        level_ref[:, :, lanes] = x_ref[:, 0:16, lanes]


def pack(atm, ocean, chunks=2):
    rows = jax.ShapeDtypeStruct((WIDE + ocean.shape[2], LANES), BF16)
    return pl.pallas_call(
        pack_kernel,
        in_specs=[HBM, HBM],
        out_specs=[VMEM] * 3,
        out_shape=[
            rows,
            rows,
            jax.ShapeDtypeStruct((2, 16, WIDE), F32),
        ],
        scratch_shapes=[
            pltpu.VMEM(atm.shape, F32),
            pltpu.VMEM(ocean.shape, F32),
            pltpu.SemaphoreType.DMA((1,)),
            pltpu.SemaphoreType.DMA((chunks,)),
        ],
        compiler_params=params(24),
        cost_estimate=cost(1 << 33, 16),
        name="pack_halo",
    )(atm, ocean)


def fetch_tiles(w_ref, tiles_ref, sems):
    count = tiles_ref.shape[0]
    first, size = w_ref.shape[0] - count, count // sems.shape[0]
    starts = [n * size for n in range(sems.shape[0])]
    return fetch(
        [(w_ref.at[pl.ds(first + t, size)], tiles_ref.at[pl.ds(t, size)]) for t in starts], sems
    )


def held_tiles(t, ahead_ref, tiles_ref, copies):
    ahead = 0 if ahead_ref is None else ahead_ref.shape[0]
    if t < ahead:
        held = ahead_ref[t : t + GROUP]
    else:
        size = tiles_ref.shape[0] // len(copies)
        if (t - ahead) % size == 0:
            copies[(t - ahead) // size].wait()
        held = tiles_ref[t - ahead : t - ahead + GROUP]
    return held.reshape(GROUP * LANES, LANES)


def forward_kernel(
    count_ref, owner_ref, block_ref, source_ref, level_ref, w_ref, out_ref, place_ref,
    picked, contrib, left,
):
    tiles = owner_ref.shape[1]
    per_row = WIDE // LANES

    source = source_ref[...]
    cell = (source & (per_row - 1)) * 16 + (source >> (per_row.bit_length() - 1))
    gather = onehot(iota((tiles, 256), 1).astype(F32) == column(cell.astype(F32)))
    for v in range(2):
        rounded = level_ref[v].astype(BF16)
        blocks = [rounded[:, b * LANES : (b + 1) * LANES] for b in range(per_row)]
        picked[v] = mxu(gather, jnp.concatenate(blocks, axis=0))
    owner = owner_ref[...].astype(F32)
    earlier = (column(owner) == owner) & (iota((tiles, tiles), 0) < iota((tiles, tiles), 1))
    rank = jnp.sum(jnp.where(earlier, 1.0, 0.0), axis=0, keepdims=True)
    live = iota((1, tiles), 1) < count_ref[...]
    place = jnp.where(live, owner_ref[...] * ROWS + rank.astype(jnp.int32), -64)
    index = jnp.where(live, owner_ref[...] * ROWS + 2 * CAP, -64)
    place_ref[0:1] = place
    place_ref[1:2] = jnp.where(live, cell, -64)
    place_ref[2:8] = jnp.zeros((6, tiles), jnp.int32)
    block = block_ref[...]
    lane = column(rank * 16.0 + ((block & 1) * 8 + (block >> 1)).astype(F32))
    names = onehot(iota((tiles, LANES), 1).astype(F32) == lane)
    part = out_ref.shape[0] * GROUP // tiles

    for t in range(0, tiles, GROUP):
        held = w_ref[t : t + GROUP].reshape(GROUP * LANES, LANES)
        row = iota((part, tiles), 0) + t // GROUP * part
        here = slice(t // GROUP * part, (t // GROUP + 1) * part)
        for m, at in enumerate((place, place + CAP, index)):
            left[here, m * tiles : (m + 1) * tiles] = onehot(row == at)
        rows = slice(t, t + GROUP)
        pair = jnp.concatenate([picked[0, rows], picked[1, rows]], axis=0)
        spread = jnp.concatenate([masked(pair, i).astype(BF16) for i in range(GROUP)], axis=1)
        both = mxu(spread, held)
        contrib[0, rows] = both[:GROUP]
        contrib[1, rows] = both[GROUP:]

    first = jnp.concatenate(split(contrib[0]), axis=1)
    second = jnp.concatenate(split(contrib[1]), axis=1)
    third = jnp.concatenate([names, jnp.zeros_like(names)], axis=1)
    out = mxu(left[...], jnp.concatenate([first, second, third], axis=0))
    out_ref[...] = out[:, :LANES] + out[:, LANES:]


def forward(count, owner, block, source, level, weights, devices):
    tiles = weights.shape[0]
    return pl.pallas_call(
        forward_kernel,
        in_specs=[VMEM] * 6,
        out_specs=[VMEM] * 2,
        out_shape=[
            jax.ShapeDtypeStruct((devices * ROWS, LANES), F32),
            jax.ShapeDtypeStruct((8, tiles), jnp.int32),
        ],
        scratch_shapes=[
            pltpu.VMEM((2, tiles, LANES), F32),
            pltpu.VMEM((2, tiles, LANES), F32),
            pltpu.VMEM((devices * ROWS, 3 * tiles), BF16),
        ],
        compiler_params=params(32),
        cost_estimate=cost(32 * tiles * LANES * LANES, 9),
        name="tiles_forward",
    )(count, owner, block, source, level, weights)


def combine_kernel(inbox_ref, ocean_ref, out_ref, flux_ref, boxes):
    devices = inbox_ref.shape[0] // ROWS

    def plane(r):
        return pl.ds(r, devices, stride=ROWS)

    names = inbox_ref[plane(6), :]
    parts = []
    for r in range(2 * CAP):
        value = inbox_ref[plane(r), :]
        high, low = split(value)
        rest = (value - high.astype(F32) - low.astype(F32)).astype(BF16)
        parts += [high, low, rest]
    summed = mxu(names.T.astype(BF16), jnp.concatenate(parts, axis=1))
    fields = []
    for v in range(2):
        received = 0.0
        for k in range(CAP):
            rows = summed[k * 16 : (k + 1) * 16]
            for term in range(3):
                at = ((v * CAP + k) * 3 + term) * LANES
                received = received + rows[:, at : at + LANES]
        surface = ocean_ref[v, 0:8]
        flux = received - jnp.concatenate([surface[:, :LANES], surface[:, LANES:]], axis=0)
        flux_ref[v] = jnp.concatenate([flux[:8], flux[8:]], axis=1)
        sent = flux.astype(BF16).astype(F32)
        empty = jnp.zeros_like(sent)
        for k in range(CAP):
            stack = [sent if j == k else empty for j in range(8)]
            fields.append(jnp.concatenate(stack, axis=0).astype(BF16))
    outgoing = mxu(names.astype(BF16), jnp.concatenate(fields, axis=1))
    for r in range(2 * CAP):
        boxes[plane(r), :] = outgoing[:, r * LANES : (r + 1) * LANES]
    for r in range(2 * CAP, ROWS):
        boxes[plane(r), :] = jnp.zeros((devices, LANES), F32)
    out_ref[...] = boxes[...].astype(BF16)


def combine(inbox, ocean):
    return pl.pallas_call(
        combine_kernel,
        in_specs=[VMEM, VMEM],
        out_specs=[VMEM, VMEM],
        out_shape=[
            jax.ShapeDtypeStruct(inbox.shape, BF16),
            jax.ShapeDtypeStruct((2, 8, 256), F32),
        ],
        scratch_shapes=[pltpu.VMEM(inbox.shape, F32)],
        compiler_params=params(24),
        name="ocean_flux",
    )(inbox, ocean)


def backward_kernel(
    place_ref, inbox_ref, w_ref, zero_ref, one_ref, _, out_ref,
    tiles_ref, picked, terms, held, sems, parts,
):
    tiles = place_ref.shape[1]
    arrivals = fetch_tiles(w_ref, tiles_ref, parts)
    per_row = WIDE // LANES
    place = column(place_ref[0:1].astype(F32)).astype(jnp.int32)
    inbox = inbox_ref[...]
    slot = iota((tiles, inbox.shape[0]), 1)
    for v in range(2):
        picked[v] = mxu(onehot(slot == place + v * CAP), inbox)
    scatter = onehot(iota((256, tiles), 0) == place_ref[1:2])

    for t in range(0, tiles, GROUP):
        weights = held_tiles(t, None, tiles_ref, arrivals)
        rows = slice(t, t + GROUP)
        pair = jnp.concatenate([picked[0, rows], picked[1, rows]], axis=0)
        wide = mxu(pair.astype(BF16), weights, ((1,), (1,)))
        both = 0.0
        for i in range(GROUP):
            both = both + masked(wide[:, i * LANES : (i + 1) * LANES], i)
        terms[0, rows] = both[:GROUP]
        terms[1, rows] = both[GROUP:]

    halves = [part for v in range(2) for part in split(terms[v])]
    summed = mxu(scatter, jnp.concatenate(halves, axis=1))
    copies = []
    for v, level_ref in enumerate((zero_ref, one_ref)):
        at = 2 * v * LANES
        returned = summed[:, at : at + LANES] + summed[:, at + LANES : at + 2 * LANES]
        for b in range(per_row):
            lanes = slice(b * LANES, (b + 1) * LANES)
            held[v, :, lanes] = level_ref[:, lanes] - couple * returned[b * 16 : (b + 1) * 16]
        copy = pltpu.make_async_copy(held.at[v], out_ref.at[v, pl.ds(0, 16)], sems.at[v])
        copy.start()
        copies.append(copy)
    for copy in copies:
        copy.wait()


def backward(place, inbox, weights, zero, one, atm, parts=4):
    tiles = weights.shape[0]
    return pl.pallas_call(
        backward_kernel,
        in_specs=[VMEM, VMEM, HBM, VMEM, VMEM, HBM],
        out_specs=HBM,
        out_shape=pltpu.HBM(atm.shape, F32),
        scratch_shapes=[
            pltpu.VMEM(weights.shape, BF16),
            pltpu.VMEM((2, tiles, LANES), F32),
            pltpu.VMEM((2, tiles, LANES), F32),
            pltpu.VMEM((2, 16, WIDE), F32),
            pltpu.SemaphoreType.DMA((2,)),
            pltpu.SemaphoreType.DMA((parts,)),
        ],
        input_output_aliases={5: 0},
        compiler_params=params(32),
        cost_estimate=cost(32 * tiles * LANES * LANES, 1),
        name="tiles_backward",
    )(place, inbox, weights, zero, one, atm)


def swap(rows):
    devices = lax.axis_size(RING)
    boxes = rows.reshape(devices, ROWS, LANES)
    return lax.all_to_all(boxes, RING, split_axis=0, concat_axis=0, tiled=True).reshape(rows.shape)


def per_device(
    atm_state,
    ocean_state,
    atm_levels,
    ocean_levels,
    tile_weight,
    tile_owner,
    tile_block,
    tile_source,
    tile_count,
):
    devices = lax.axis_size(RING)
    tiles = tile_weight.shape[0]
    atm = atm_state.reshape(2, 256, WIDE)
    ocean = ocean_state.reshape(2, 128, 256)
    grp, dom = lax.axis_index("grp"), lax.axis_index("dom")
    last = lax.axis_size("dom") - 1
    edge = jnp.stack([grp, (dom == 0).astype(jnp.int32), (dom == last).astype(jnp.int32)])

    atm = pltpu.with_memory_space_constraint(atm, pltpu.HBM)
    sea_state = pltpu.with_memory_space_constraint(ocean, pltpu.HBM)
    again = pltpu.with_memory_space_constraint(tile_weight, pltpu.HBM)
    lists = [x.reshape(1, tiles) for x in (tile_owner, tile_block, tile_source)]
    to_next, to_prev, level = pack(atm, sea_state)
    forth = [(i, (i + 1) % devices) for i in range(devices)]
    back = [(target, source) for source, target in forth]
    low = lax.ppermute(to_next, RING, forth)
    high = lax.ppermute(to_prev, RING, back)
    outbox, place = forward(
        tile_count.reshape(1, 1), *lists, level, tile_weight, devices
    )
    inbox = swap(outbox)
    columns = edge_rows(edge, ocean, low, high)
    side = lax.ppermute(columns, "grp", [(0, 1), (1, 0)])
    half, zero, halo, sea, own = early(edge, atm_levels, ocean_levels, atm, low, high)
    own = pltpu.with_memory_space_constraint(own, pltpu.HBM)
    inbox, half, side = lax.optimization_barrier((inbox, half, side))
    outgoing, flux = combine(inbox, ocean)
    returned = swap(outgoing)
    whole, one, ocean_final = late(
        edge, atm, ocean, low, high, side, flux, halo, sea, own, half
    )
    returned, whole, ocean_final = lax.optimization_barrier((returned, whole, ocean_final))
    atm_final = backward(place, returned, again, zero, one, whole)
    return atm_final.reshape(atm_state.shape), ocean_final.reshape(ocean_state.shape)


def solution(mesh):
    in_specs = (
        P(None, None, RING, None),
        P(None, None, "dom", "grp"),
        P(),
        P(),
        P(RING, None, None),
        P(RING, None),
        P(RING),
        P(RING),
        P(RING),
    )
    out_specs = (P(None, None, RING, None), P(None, None, "dom", "grp"))
    return jax.shard_map(
        per_device, mesh=mesh, in_specs=in_specs, out_specs=out_specs, check_vma=False
    )
```
